128 devices in a mesh: layer: 2 (over core), prow: 4 (over x), pcol: 16 (over z, y).
Axes of the slice: x: 4, y: 4, z: 4, core: 2. Of those that a mesh axis runs over, the one named last changes fastest.
Arguments:
- stored_inverse: bfloat16 [8192, 8192], P('prow', 'pcol'), may hold values from -4 to 64, as said below
- lhat: bfloat16 [2, 4096, 256], P('layer', ('prow', 'pcol')), may hold values from -0.25 to 0.25
- diag_inverse: bfloat16 [2, 2, 256, 256], P('layer'), may hold values from -6 to 6
- ancestors: int32 [2, 2, 8], P('layer'), may hold values from 0 to 29, as said below
Outputs:
- column_blocks: bfloat16 [2, 8192, 512], P('layer', 'prow')
- row_blocks: bfloat16 [2, 8192, 512], P('layer', 'pcol')
- diag_blocks: bfloat16 [2, 2, 256, 256], P('layer')
The draws below stay inside these ranges and needn't reach their ends.
Inputs may be any that keep to these rules, and one draw needn't show every extreme that they name: `stored_inverse`: Symmetric; every tile whose row or column block index is 28 or more is zero. `ancestors`: each list holds 8 distinct block indices in increasing order. At level 0 they are below 28. At level l >= 1 the list of a supernode is its parent's list (the parent is a supernode of level l - 1) with one entry removed, followed by the parent's own block; every supernode of level l - 1 is the parent of exactly one supernode of level l.
All inputs are finite; a program needn't handle non-finite values.
Results may differ from the reference program's by a relative error of at most 0.018.
Values may be sent and summed in bfloat16 or wider, within the bound.
A program may use at most 128 MiB of HBM per device.

```python
import math
import jax
import jax.numpy as jnp
from jax import lax

BLOCK = 256
ANCESTORS = 8
SUPERS = 2
BLOCKS = 32
LEVELS = 2
TOP_BLOCKS = 28
N_PROW = 4
N_PCOL = 16


def draw_stored_inverse(key, part):
    key = jax.random.fold_in(key, 5)
    order_size = BLOCKS * BLOCK
    top_rows = TOP_BLOCKS * BLOCK
    noise_draw = jax.random.truncated_normal(jax.random.fold_in(key, 1), -4.0, 4.0, (order_size, order_size), jnp.float32)
    spread = 0.5 / math.sqrt(ANCESTORS * BLOCK)
    symmetric = (noise_draw + noise_draw.T) * (0.7071 * spread)
    diagonal = jnp.exp(jax.random.uniform(jax.random.fold_in(key, 2), (order_size,), jnp.float32, 0.0, math.log(4.0)))
    positions = jnp.arange(order_size)
    matrix = jnp.where(positions[:, None] == positions[None, :], diagonal[:, None], symmetric)
    inside = positions < top_rows
    matrix = jnp.where(inside[:, None] & inside[None, :], matrix, 0.0)
    return matrix.astype(jnp.bfloat16)


def draw_ancestors(key, part):
    key = jax.random.fold_in(key, 7)
    first_lists = []
    for super_id in range(SUPERS):
        if super_id == 0:
            others = jax.random.permutation(jax.random.fold_in(key, 100 + super_id), TOP_BLOCKS - 1)[:ANCESTORS - 1] + 1
            shuffled = jnp.concatenate([jnp.zeros((1,), jnp.int32), others.astype(jnp.int32)])
        else:
            shuffled = jax.random.permutation(jax.random.fold_in(key, 100 + super_id), TOP_BLOCKS)[:ANCESTORS]
        first_lists.append(jnp.sort(shuffled.astype(jnp.int32)))
    current = jnp.stack(first_lists).astype(jnp.int32)
    level_lists = [current]
    slots = jnp.arange(ANCESTORS - 1, dtype=jnp.int32)
    for level in range(1, LEVELS):
        rotation = jax.random.randint(jax.random.fold_in(key, 200 + level), (), 0, SUPERS)
        parents = ((jnp.arange(SUPERS, dtype=jnp.int32) + rotation) % SUPERS).astype(jnp.int32)
        dropped = jax.random.randint(jax.random.fold_in(key, 300 + level), (SUPERS,), 0, ANCESTORS)
        kept_index = slots[None, :] + (slots[None, :] >= dropped[:, None]).astype(jnp.int32)
        kept = jnp.take_along_axis(current[parents], kept_index, axis=1)
        parent_block = TOP_BLOCKS + (level - 1) * SUPERS + parents
        current = jnp.concatenate([kept, parent_block[:, None]], axis=1).astype(jnp.int32)
        level_lists.append(current)
    return jnp.stack(level_lists).astype(jnp.int32)


def block_scale(rng, extent, shards, least, top_value):
    gain, own = 1.0, jax.random.fold_in(rng, 6)
    for axis_at, blocks in shards:
        steps = jnp.exp(jax.random.uniform(jax.random.fold_in(own, axis_at), (blocks,), jnp.float32, least / len(shards), top_value / len(shards)))
        gain = gain * jnp.repeat(steps, extent[axis_at] // blocks).reshape([-1 if axis == axis_at else 1 for axis in range(len(extent))])
    return gain


def bell_draw(stream_key, dims, scale, limit, shards=(), held_as=jnp.bfloat16):
    gain = block_scale(stream_key, dims, shards, -0.22, 0.18) if shards else 1.0
    array = jax.random.normal(stream_key, dims, jnp.float32) * scale * gain
    return jnp.minimum(jnp.maximum(array, -limit), limit).astype(held_as)


def setup_inputs(seed: int = 0) -> dict:
    key_list = jax.random.split(jax.random.key(seed), 5)
    return {
        "stored_inverse": draw_stored_inverse(jax.random.fold_in(key_list[4], 71), 0),
        "lhat": bell_draw(key_list[1], (LEVELS, SUPERS * ANCESTORS * BLOCK, BLOCK), (2 * BLOCK) ** -0.5, 0.25, ((0, 2), (1, 64))),
        "diag_inverse": bell_draw(key_list[2], (LEVELS, SUPERS, BLOCK, BLOCK), 1.0, 6.0, ((0, 2),)),
        "ancestors": draw_ancestors(jax.random.fold_in(key_list[4], 71), 0),
    }


def grouped(term_stack, group_ids, group_count):
    total = jnp.zeros(term_stack.shape[1:], jnp.float32)
    for group in range(group_count):
        part_sum = jnp.sum(jnp.where((group_ids == group)[:, None, None], term_stack, 0.0), axis=0)
        rounded = lax.optimization_barrier(part_sum.astype(jnp.bfloat16))
        total = total + rounded.astype(jnp.float32)
    return total


def reference(stored_inverse, lhat, diag_inverse, ancestors):
    row_range = BLOCKS // N_PROW
    col_range = BLOCKS // N_PCOL
    matrix = stored_inverse
    block_index = jnp.arange(BLOCKS, dtype=jnp.int32)
    column_levels, row_levels, diag_levels = [], [], []
    for level in range(LEVELS):
        panel_tiles = lhat[level].reshape(SUPERS, ANCESTORS, BLOCK, BLOCK)
        column_list, row_list, diag_list = [], [], []
        for super_id in range(SUPERS):
            anc_list = ancestors[level, super_id].astype(jnp.int32)
            member = jnp.repeat(jnp.any(anc_list[:, None] == block_index[None, :], axis=0), BLOCK)
            col_terms = jnp.stack([jnp.dot(lax.dynamic_slice_in_dim(matrix, (anc_list[slot] * BLOCK).astype(jnp.int32), BLOCK, 1), panel_tiles[super_id, slot], preferred_element_type=jnp.float32) for slot in range(ANCESTORS)])
            row_terms = jnp.stack([jnp.dot(lax.dynamic_slice_in_dim(matrix, (anc_list[slot] * BLOCK).astype(jnp.int32), BLOCK, 0).T, panel_tiles[super_id, slot], preferred_element_type=jnp.float32) for slot in range(ANCESTORS)])
            column_value = grouped(col_terms, anc_list // col_range, N_PCOL)
            row_value = grouped(row_terms, anc_list // row_range, N_PROW)
            x_column = jnp.where(member[:, None], -column_value, 0.0).astype(jnp.bfloat16)
            y_column = jnp.where(member[:, None], -row_value, 0.0).astype(jnp.bfloat16)
            diag_terms = jnp.stack([jnp.dot(panel_tiles[super_id, slot].T, lax.dynamic_slice_in_dim(x_column, (anc_list[slot] * BLOCK).astype(jnp.int32), BLOCK, 0), preferred_element_type=jnp.float32) for slot in range(ANCESTORS)])
            diag_value = (diag_inverse[level, super_id].astype(jnp.float32) - jnp.sum(diag_terms, axis=0)).astype(jnp.bfloat16)
            column_list.append(x_column)
            row_list.append(y_column)
            diag_list.append(diag_value)
        for super_id in range(SUPERS):
            first_row = (TOP_BLOCKS + level * SUPERS + super_id) * BLOCK
            matrix = matrix.at[:, first_row:first_row + BLOCK].set(column_list[super_id])
            matrix = matrix.at[first_row:first_row + BLOCK, :].set(row_list[super_id].T)
            matrix = matrix.at[first_row:first_row + BLOCK, first_row:first_row + BLOCK].set(diag_list[super_id])
        column_levels.append(jnp.concatenate(column_list, axis=1))
        row_levels.append(jnp.concatenate(row_list, axis=1))
        diag_levels.append(jnp.stack(diag_list))
    return jnp.stack(column_levels), jnp.stack(row_levels), jnp.stack(diag_levels)
```

```python
import functools

import jax
import jax.numpy as jnp
from jax import lax
from jax.experimental import pallas as pl
from jax.experimental.pallas import tpu as pltpu
from jax.sharding import PartitionSpec as P

BLOCK = 256
ANCESTORS = 8
SUPERS = 2
TOP_BLOCKS = 28
SIDE = 4
PLANE = 16
QUARTER = 64
SLOTS = SUPERS * ANCESTORS
MESH = pl.DeviceIdType.MESH
BF16 = jnp.bfloat16
F32 = jnp.float32

ROUTES = (
    (("y", "z", "x"), (0, 48), (0, 128)),
    (("x", "z", "y"), (0, 48), (128, 128)),
    (("x", "y", "z"), (48, 16), (0, 256)),
)
HOPS = (2, 1, 3)


def kernel(
    anc, anc_v, panel, g_any, dinv,
    col_out, row_out, diag_out,
    panels, g_own, g_pick, panel_t, partial, partial_in, summed, staged, moved, slots, sibling_slots,
    sibling_diag, diag_send, tiles, anc_in, anc_other,
    g_sem, anc_send, anc_recv, anc_local,
    send1, recv1, send2, recv2, x_send, x_recv, c_send, c_recv, a_send, a_recv, d_send, d_recv,
):
    layer = lax.axis_index("layer")
    x = lax.axis_index("prow")
    c = lax.axis_index("pcol")
    z = c // SIDE
    y = c % SIDE
    me = {"x": x, "y": y, "z": z}

    def device(at, on_layer=None):
        return (layer if on_layer is None else on_layer, at["x"], at["z"] * SIDE + at["y"])

    g_copy = pltpu.make_async_copy(g_any, g_own, g_sem)
    g_copy.start()

    barrier = pltpu.get_barrier_semaphore()

    def greet_plane(step, carry):
        pl.semaphore_signal(barrier, inc=1, device_id=(layer, x, (c + step) % PLANE), device_id_type=MESH)
        return carry

    def greet_line(step, carry):
        pl.semaphore_signal(barrier, inc=1, device_id=(layer, (x + step) % SIDE, c), device_id_type=MESH)
        return carry

    lax.fori_loop(1, PLANE, greet_plane, 0)
    lax.fori_loop(1, SIDE, greet_line, 0)
    pl.semaphore_signal(barrier, inc=1, device_id=(1 - layer, x, c), device_id_type=MESH)
    pl.semaphore_wait(barrier, PLANE - 1 + SIDE - 1 + 1)

    anc_copy = pltpu.make_async_remote_copy(
        src_ref=anc_v, dst_ref=anc_in, send_sem=anc_send, recv_sem=anc_recv,
        device_id=(1 - layer, x, c), device_id_type=MESH,
    )
    anc_copy.start()

    def gather_phase(buf, dims, phase, route, send, recv):
        order, rows, cols = ROUTES[route]
        index = tuple(pl.ds(0, SIDE) if d in order[:phase] else me[d] for d in dims)
        part = buf.at[index + (pl.ds(*rows), pl.ds(*cols))]
        axis = order[phase]
        copies = []
        for hop in HOPS:
            at = dict(me)
            at[axis] = (me[axis] + hop) % SIDE
            copies.append(pltpu.make_async_remote_copy(
                src_ref=part, dst_ref=part,
                send_sem=send.at[route, phase, hop - 1], recv_sem=recv.at[route, phase, hop - 1],
                device_id=device(at), device_id_type=MESH,
            ))
        return copies

    def gather(buf, dims, send, recv, beside=None):
        sent = []
        for phase in range(3):
            now = [gather_phase(buf, dims, phase, route, send, recv) for route in range(3)]
            if phase == 0:
                for copies in now:
                    for copy in copies:
                        copy.start()
            sent.append(now)
            if phase == 0 and beside is not None:
                beside()
            for route in range(3):
                for copy in sent[phase][route]:
                    copy.wait_recv()
                if phase < 2:
                    ahead = gather_phase(buf, dims, phase + 1, route, send, recv)
                    for copy in ahead:
                        copy.start()
        for now in sent:
            for copies in now:
                for copy in copies:
                    copy.wait_send()

    panels[x, z, y] = panel[0]

    def pick_blocks():
        g_copy.wait()
        for k in range(SUPERS):
            def pick(p, carry):
                at = anc[0, k, p] - x * ANCESTORS
                here = jnp.logical_and(at >= 0, at < ANCESTORS)
                block = g_own[jnp.clip(at, 0, ANCESTORS - 1)]
                block = jnp.where(here, block, jnp.zeros_like(block))
                turned = block.T
                for b in range(2):
                    for q in range(SIDE):
                        first = b * BLOCK + q * QUARTER
                        g_pick[k, p, q, b] = turned[first:first + QUARTER]
                return carry
            lax.fori_loop(0, ANCESTORS, pick, 0)

    gather(panels, ("x", "z", "y"), send1, recv1, pick_blocks)

    for k in range(SUPERS):
        total = jnp.zeros((2 * BLOCK, BLOCK), F32)
        for p in range(ANCESTORS):
            tile = panels[2 * k + p // SIDE, p % SIDE].reshape(BLOCK, BLOCK)
            total += jnp.dot(
                g_pick[k, p].reshape(2 * BLOCK, BLOCK), tile, preferred_element_type=F32
            )
        partial[:, k] = total.astype(BF16).reshape(SIDE, 2, QUARTER, BLOCK)

    x_copies = []
    for hop in HOPS:
        to = (x + hop) % SIDE
        x_copies.append(pltpu.make_async_remote_copy(
            src_ref=partial.at[to], dst_ref=partial_in.at[hop - 1],
            send_sem=x_send.at[hop - 1], recv_sem=x_recv.at[hop - 1],
            device_id=(layer, to, c), device_id_type=MESH,
        ))
    for copy in x_copies:
        copy.start()
    for k in range(SUPERS):
        def turn(p, carry):
            panel_t[k, p] = panels[2 * k + p // SIDE, p % SIDE].reshape(BLOCK, BLOCK).T
            return carry
        lax.fori_loop(0, ANCESTORS, turn, 0)
    for copy in x_copies:
        copy.wait_recv()
    total = partial[x].astype(F32)
    for hop in HOPS:
        total += partial_in[hop - 1].astype(F32)
    summed[...] = total.astype(BF16)

    for s in range(SLOTS):
        at = jnp.clip(anc[0, s // ANCESTORS, s % ANCESTORS] - 2 * c, 0, 1)
        staged[s] = summed[s // ANCESTORS, at]

    def to_slot(step):
        to = (c + step) % PLANE
        return pltpu.make_async_remote_copy(
            src_ref=staged.at[to], dst_ref=moved.at[c],
            send_sem=c_send.at[step], recv_sem=c_recv.at[step],
            device_id=(layer, x, to), device_id_type=MESH,
        )

    def start_slot(step, carry):
        to_slot(step).start()
        return carry

    def wait_slot(step, carry):
        to_slot(step).wait_recv()
        return carry

    lax.fori_loop(1, PLANE, start_slot, 0)
    moved[c] = staged[c]
    lax.fori_loop(1, PLANE, wait_slot, 0)
    holder = anc[0, c // ANCESTORS, c % ANCESTORS] // 2
    slots[z, y, x] = moved[holder]
    gather(slots, ("z", "y", "x"), send2, recv2)

    a_copy = pltpu.make_async_remote_copy(
        src_ref=slots, dst_ref=sibling_slots, send_sem=a_send, recv_sem=a_recv,
        device_id=(1 - layer, x, c), device_id_type=MESH,
    )
    d_copy = pltpu.make_async_remote_copy(
        src_ref=diag_send, dst_ref=sibling_diag, send_sem=d_send, recv_sem=d_recv,
        device_id=(1 - layer, x, c), device_id_type=MESH,
    )
    anc_copy.wait_recv()
    to_smem = pltpu.make_async_copy(anc_in, anc_other, anc_local)
    to_smem.start()
    to_smem.wait()

    def slot_tile(ref, s):
        return ref[s // SIDE, s % SIDE].reshape(BLOCK, BLOCK)

    @pl.when(layer == 0)
    def _():
        a_copy.start()
        for k in range(SUPERS):
            total = dinv[0, k].astype(F32)
            for q in range(ANCESTORS):
                total += jnp.dot(
                    panel_t[k, q], slot_tile(slots, k * ANCESTORS + q), preferred_element_type=F32
                )
            diag_send[k] = total.astype(BF16)
            diag_out[0, k] = total.astype(BF16)
        d_copy.start()
        for k in range(SUPERS):
            for q in range(ANCESTORS):
                tiles[k, q] = -slot_tile(slots, k * ANCESTORS + q)
            tiles[k, ANCESTORS] = jnp.zeros((BLOCK, BLOCK), BF16)
        a_copy.wait_send()
        d_copy.wait_send()

    @pl.when(layer == 1)
    def _():
        a_copy.wait_recv()
        last = ANCESTORS - 1
        turned_sum = []
        for k in range(SUPERS):
            parent = jnp.clip(anc[0, k, last] - TOP_BLOCKS, 0, SUPERS - 1)
            edge = panels[2 * k + 1, SIDE - 1].reshape(BLOCK, BLOCK)
            total = jnp.zeros((BLOCK, BLOCK), F32)
            for q in range(last):
                block = anc[0, k, q]
                at = jnp.int32(0)
                for j in range(ANCESTORS):
                    at = jnp.where(anc_other[0, parent, j] == block, j, at)
                s = parent * ANCESTORS + at
                tile = sibling_slots[s // SIDE, s % SIDE].reshape(BLOCK, BLOCK)
                total += jnp.dot(panel_t[k, q], tile, preferred_element_type=F32)
                new = jnp.dot(tile, edge, preferred_element_type=F32)
                tiles[k, q] = (new - slot_tile(slots, k * ANCESTORS + q).astype(F32)).astype(BF16)
            turned_sum.append(total.T)
        d_copy.wait_recv()
        for k in range(SUPERS):
            parent = jnp.clip(anc[0, k, last] - TOP_BLOCKS, 0, SUPERS - 1)
            edge = panels[2 * k + 1, SIDE - 1].reshape(BLOCK, BLOCK)
            above = sibling_diag[parent]
            tiles[k, last] = (
                turned_sum[k] - jnp.dot(above, edge, preferred_element_type=F32)
            ).astype(BF16)
            tiles[k, ANCESTORS] = (
                turned_sum[k] - jnp.dot(above.T, edge, preferred_element_type=F32)
            ).astype(BF16)
            total = dinv[0, k].astype(F32)
            for q in range(ANCESTORS):
                total -= jnp.dot(panel_t[k, q], tiles[k, q], preferred_element_type=F32)
            diag_out[0, k] = total.astype(BF16)

    def place(out, first, blocks, row_side):
        for k in range(SUPERS):
            def put(j, carry):
                at = jnp.int32(0)
                hit = jnp.int32(0)
                for q in range(ANCESTORS):
                    same = anc[0, k, q] == first + j
                    at = jnp.where(same, q, at)
                    hit = jnp.where(same, 1, hit)
                if row_side:
                    turned = jnp.logical_and(layer == 1, at == ANCESTORS - 1)
                    at = jnp.where(turned, ANCESTORS, at)
                tile = tiles[k, at]
                start = pl.multiple_of(j * BLOCK, BLOCK)
                out[0, pl.ds(start, BLOCK), k * BLOCK:(k + 1) * BLOCK] = jnp.where(
                    hit > 0, tile, jnp.zeros_like(tile)
                )
                return carry
            lax.fori_loop(0, blocks, put, 0)

    place(col_out, x * ANCESTORS, ANCESTORS, False)
    place(row_out, c * 2, 2, True)

    anc_copy.wait_send()
    for copy in x_copies:
        copy.wait_send()

    def sent_slot(step, carry):
        to_slot(step).wait_send()
        return carry

    lax.fori_loop(1, PLANE, sent_slot, 0)


def body(stored_inverse, lhat, diag_inverse, ancestors):
    rows, cols = stored_inverse.shape
    stored = stored_inverse.reshape(rows // BLOCK, BLOCK, cols)
    vmem = pl.BlockSpec(memory_space=pltpu.VMEM)
    dma = pltpu.SemaphoreType.DMA
    width = SUPERS * BLOCK
    return pl.pallas_call(
        kernel,
        out_shape=(
            jax.ShapeDtypeStruct((1, rows, width), BF16),
            jax.ShapeDtypeStruct((1, cols, width), BF16),
            jax.ShapeDtypeStruct(diag_inverse.shape, BF16),
        ),
        in_specs=[pl.BlockSpec(memory_space=pltpu.SMEM), vmem, vmem, pl.BlockSpec(memory_space=pl.ANY), vmem],
        out_specs=(vmem, vmem, vmem),
        scratch_shapes=[
            pltpu.VMEM((SIDE, SIDE, SIDE, QUARTER, BLOCK), BF16),
            pltpu.VMEM((rows // BLOCK, BLOCK, cols), BF16),
            pltpu.VMEM((SUPERS, ANCESTORS, SIDE, 2, QUARTER, BLOCK), BF16),
            pltpu.VMEM((SUPERS, ANCESTORS, BLOCK, BLOCK), BF16),
            pltpu.VMEM((SIDE, SUPERS, 2, QUARTER, BLOCK), BF16),
            pltpu.VMEM((SIDE - 1, SUPERS, 2, QUARTER, BLOCK), BF16),
            pltpu.VMEM((SUPERS, 2, QUARTER, BLOCK), BF16),
            pltpu.VMEM((SLOTS, QUARTER, BLOCK), BF16),
            pltpu.VMEM((PLANE, QUARTER, BLOCK), BF16),
            pltpu.VMEM((SIDE, SIDE, SIDE, QUARTER, BLOCK), BF16),
            pltpu.VMEM((SIDE, SIDE, SIDE, QUARTER, BLOCK), BF16),
            pltpu.VMEM((SUPERS, BLOCK, BLOCK), BF16),
            pltpu.VMEM((SUPERS, BLOCK, BLOCK), BF16),
            pltpu.VMEM((SUPERS, ANCESTORS + 1, BLOCK, BLOCK), BF16),
            pltpu.VMEM((1, SUPERS, ANCESTORS), jnp.int32),
            pltpu.SMEM((1, SUPERS, ANCESTORS), jnp.int32),
            dma, dma, dma, dma,
            dma((3, 3, 3)), dma((3, 3, 3)), dma((3, 3, 3)), dma((3, 3, 3)),
            dma((3,)), dma((3,)), dma((PLANE,)), dma((PLANE,)),
            dma, dma, dma, dma,
        ],
        compiler_params=pltpu.CompilerParams(
            collective_id=0, has_side_effects=True, vmem_limit_bytes=48 << 20
        ),
        name="selected_inverse",
    )(ancestors, ancestors, lhat, stored, diag_inverse)


def solution(mesh):
    return jax.shard_map(
        body,
        mesh=mesh,
        in_specs=(
            P("prow", "pcol"),
            P("layer", ("prow", "pcol"), None),
            P("layer", None, None, None),
            P("layer", None, None),
        ),
        out_specs=(
            P("layer", "prow", None),
            P("layer", "pcol", None),
            P("layer", None, None, None),
        ),
        check_vma=False,
    )
```

```python
import functools

import jax
import jax.numpy as jnp
from jax import lax
from jax.experimental import pallas as pl
from jax.experimental.pallas import tpu as pltpu
from jax.sharding import PartitionSpec as P

BLOCK = 256
ANCESTORS = 8
SUPERS = 2
TOP_BLOCKS = 28
SIDE = 4
PLANE = 16
QUARTER = 64
HALVES = 2
HALF = BLOCK // HALVES
SLOTS = SUPERS * ANCESTORS
MESH = pl.DeviceIdType.MESH
BF16 = jnp.bfloat16
F32 = jnp.float32
VMEM_LIMIT = 64 << 20

ROUTES = (
    ((("y", "z", "x"), 0, 32), (("x", "z", "y"), 32, 32)),
    ((("y", "z", "x"), 0, 16), (("z", "x", "y"), 16, 16), (("x", "y", "z"), 32, 32)),
)
HOPS = (2, 1, 3)
LINKS = 56


class Gather:
    def __init__(self, buf, dims, me, layer, routes, send, recv):
        self.buf, self.dims, self.me, self.layer, self.routes = buf, dims, me, layer, routes
        self.send, self.recv = send, recv
        self.count = 0
        self.sent, self.second, self.third = [], [], []

    def copies(self, route, full, axis, fixed=None):
        _, first, rows = route
        fixed = fixed or {}
        index = tuple(
            fixed[d] if d in fixed else pl.ds(0, SIDE) if d in full else self.me[d]
            for d in self.dims
        )
        part = self.buf.at[index + (pl.ds(first, rows),)]
        made = []
        for hop in HOPS:
            at = dict(self.me)
            at[axis] = (self.me[axis] + hop) % SIDE
            copy = pltpu.make_async_remote_copy(
                src_ref=part, dst_ref=part,
                send_sem=self.send.at[self.count], recv_sem=self.recv.at[self.count],
                device_id=(self.layer, at["x"], at["z"] * SIDE + at["y"]), device_id_type=MESH,
            )
            self.count += 1
            copy.start()
            made.append(copy)
        self.sent += made
        return made

    def start(self):
        self.first = [self.copies(route, (), route[0][0]) for route in self.routes]

    def after_first(self):
        for route, arriving in zip(self.routes, self.first):
            order = route[0]
            for copy in arriving:
                copy.wait_recv()
            self.second.append(self.copies(route, order[:1], order[1]))
        for route in self.routes:
            order = route[0]
            self.third += self.copies(route, order[:1], order[2])

    def after_second(self):
        for n, hop in enumerate(HOPS):
            for route, arriving in zip(self.routes, self.second):
                order = route[0]
                arriving[n].wait_recv()
                came_from = (self.me[order[1]] + SIDE - hop) % SIDE
                self.third += self.copies(route, order[:1], order[2], {order[1]: came_from})

    def finish(self):
        for copy in self.third:
            copy.wait_recv()

    def wait_sent(self):
        for copy in self.sent:
            copy.wait_send()


def kernel(
    anc_any, panel_any, g_any, dinv_any,
    tiles_out, diag_out,
    anc, dinv, panels, g_own, g_pick, panel_t, partial, partial_in, summed, staged, moved0, moved1, slots,
    sibling_slots0, sibling_slots1, sibling_diag, diag_send, tiles, diag, anc_in, anc_other,
    g_sem, in_sem, anc_send, anc_recv, anc_local,
    send1, recv1, send2, recv2, x_send, x_recv, c_send, c_recv, a_send, a_recv, d_send, d_recv, out_sem,
):
    layer = lax.axis_index("layer")
    x = lax.axis_index("prow")
    c = lax.axis_index("pcol")
    z = c // SIDE
    y = c % SIDE
    me = {"x": x, "y": y, "z": z}
    halves = range(HALVES)
    last = ANCESTORS - 1
    moved = (moved0, moved1)
    sibling_slots = (sibling_slots0, sibling_slots1)

    in_copies = [
        pltpu.make_async_copy(
            panel_any.at[0, :, pl.ds(h * HALF, HALF)], panels.at[h, x, z, y], in_sem.at[h]
        )
        for h in halves
    ]
    anc_load = pltpu.make_async_copy(anc_any, anc, in_sem.at[2])
    dinv_load = pltpu.make_async_copy(dinv_any, dinv, in_sem.at[3])
    g_load = pltpu.make_async_copy(g_any, g_own, g_sem)
    for copy in in_copies:
        copy.start()
    anc_load.start()
    g_load.start()
    dinv_load.start()

    barrier = pltpu.get_barrier_semaphore()

    def greet_plane(step, carry):
        pl.semaphore_signal(barrier, inc=1, device_id=(layer, x, (c + step) % PLANE), device_id_type=MESH)
        return carry

    def greet_line(step, carry):
        pl.semaphore_signal(barrier, inc=1, device_id=(layer, (x + step) % SIDE, c), device_id_type=MESH)
        return carry

    lax.fori_loop(1, PLANE, greet_plane, 0)
    lax.fori_loop(1, SIDE, greet_line, 0)
    pl.semaphore_signal(barrier, inc=1, device_id=(1 - layer, x, c), device_id_type=MESH)
    pl.semaphore_wait(barrier, PLANE - 1 + SIDE - 1 + 1)

    gather1 = [
        Gather(panels.at[h], ("x", "z", "y"), me, layer, ROUTES[h], send1.at[h], recv1.at[h])
        for h in halves
    ]
    gather2 = [
        Gather(slots.at[h], ("z", "y", "x"), me, layer, ROUTES[h], send2.at[h], recv2.at[h])
        for h in halves
    ]
    for copy in in_copies:
        copy.wait()
    gather1[0].start()
    sibling = (1 - layer, x, c)
    anc_copy = pltpu.make_async_remote_copy(
        src_ref=anc_any, dst_ref=anc_in, send_sem=anc_send, recv_sem=anc_recv,
        device_id=sibling, device_id_type=MESH,
    )
    anc_copy.start()
    anc_load.wait()
    g_load.wait()
    dinv_load.wait()

    def pick_blocks(k):
        def pick(p, carry):
            at = anc[0, k, p] - x * ANCESTORS
            here = jnp.logical_and(at >= 0, at < ANCESTORS)
            block = g_own[jnp.clip(at, 0, ANCESTORS - 1)]
            block = jnp.where(here, block, jnp.zeros_like(block))
            turned = block.T
            for b in range(2):
                for q in range(SIDE):
                    first = b * BLOCK + q * QUARTER
                    g_pick[k, p, q, b] = turned[first:first + QUARTER]
            return carry
        lax.fori_loop(0, ANCESTORS, pick, 0)

    def panel_tile(h, k, p):
        return panels[h, 2 * k + p // SIDE, p % SIDE].reshape(BLOCK, HALF)

    def multiply(h):
        for k in range(SUPERS):
            total = jnp.zeros((2 * BLOCK, HALF), F32)
            for p in range(ANCESTORS):
                total += jnp.dot(
                    g_pick[k, p].reshape(2 * BLOCK, BLOCK), panel_tile(h, k, p),
                    preferred_element_type=F32,
                )
            partial[h, :, k] = total.astype(BF16).reshape(SIDE, 2, QUARTER, HALF)

    x_copies = [[], []]

    def start_reduce(h):
        for hop in HOPS:
            to = (x + hop) % SIDE
            copy = pltpu.make_async_remote_copy(
                src_ref=partial.at[h, to], dst_ref=partial_in.at[h, hop - 1],
                send_sem=x_send.at[h, hop - 1], recv_sem=x_recv.at[h, hop - 1],
                device_id=(layer, to, c), device_id_type=MESH,
            )
            copy.start()
            x_copies[h].append(copy)

    def turn_panels(h):
        for k in range(SUPERS):
            for p in range(ANCESTORS):
                panel_t[k, p, h * HALF:(h + 1) * HALF, :] = panel_tile(h, k, p).T

    def to_slot(h, step):
        to = (c + step) % PLANE
        return pltpu.make_async_remote_copy(
            src_ref=staged.at[h, to], dst_ref=moved[h].at[c],
            send_sem=c_send.at[h, step], recv_sem=c_recv.at[h, step],
            device_id=(layer, x, to), device_id_type=MESH,
        )

    def each_slot(h, act):
        def step_of(step, carry):
            act(to_slot(h, step))
            return carry
        lax.fori_loop(1, PLANE, step_of, 0)

    def start_move(h):
        for copy in x_copies[h]:
            copy.wait_recv()
        total = partial[h, x].astype(F32)
        for hop in HOPS:
            total += partial_in[h, hop - 1].astype(F32)
        summed[h] = total.astype(BF16)
        for s in range(SLOTS):
            at = jnp.clip(anc[0, s // ANCESTORS, s % ANCESTORS] - 2 * c, 0, 1)
            staged[h, s] = summed[h, s // ANCESTORS, at]
        each_slot(h, lambda copy: copy.start())
        moved[h][c] = staged[h, c]

    def end_move(h):
        each_slot(h, lambda copy: copy.wait_recv())
        holder = anc[0, c // ANCESTORS, c % ANCESTORS] // 2
        slots[h, z, y, x] = moved[h][holder]

    def a_copy(h):
        return pltpu.make_async_remote_copy(
            src_ref=slots.at[h], dst_ref=sibling_slots[h], send_sem=a_send.at[h], recv_sem=a_recv.at[h],
            device_id=sibling, device_id_type=MESH,
        )

    def d_copy(h):
        return pltpu.make_async_remote_copy(
            src_ref=diag_send.at[h], dst_ref=sibling_diag.at[h], send_sem=d_send.at[h], recv_sem=d_recv.at[h],
            device_id=sibling, device_id_type=MESH,
        )

    def slot_tile(ref, s):
        return ref[s // SIDE, s % SIDE].reshape(BLOCK, HALF)

    def out_copy(k, first, count):
        return pltpu.make_async_copy(
            tiles.at[k, pl.ds(first, count)], tiles_out.at[k, pl.ds(first, count)],
            out_sem.at[k, first // last],
        )

    diag_store = pltpu.make_async_copy(diag, diag_out, out_sem.at[2, 0])

    pick_blocks(0)
    gather1[0].after_first()
    gather1[1].start()
    pick_blocks(1)
    gather1[0].after_second()
    gather1[1].after_first()
    gather1[0].finish()
    gather1[1].after_second()
    multiply(0)
    start_reduce(0)
    turn_panels(0)
    gather1[1].finish()
    multiply(1)
    start_reduce(1)
    start_move(0)
    turn_panels(1)
    start_move(1)
    end_move(0)
    gather2[0].start()
    anc_copy.wait_recv()
    to_smem = pltpu.make_async_copy(anc_in, anc_other, anc_local)
    to_smem.start()
    to_smem.wait()
    gather2[0].after_first()
    end_move(1)
    gather2[1].start()
    gather2[0].after_second()
    gather2[1].after_first()
    gather2[0].finish()

    @pl.when(layer == 0)
    def _():
        a_copy(0).start()

    gather2[1].after_second()

    @pl.when(layer == 0)
    def _():
        def half(h):
            for k in range(SUPERS):
                total = dinv[0, k, :, h * HALF:(h + 1) * HALF].astype(F32)
                for q in range(ANCESTORS):
                    total += jnp.dot(
                        panel_t[k, q], slot_tile(slots.at[h], k * ANCESTORS + q),
                        preferred_element_type=F32,
                    )
                diag_send[h, k] = total.astype(BF16)
                diag[0, k, :, h * HALF:(h + 1) * HALF] = total.astype(BF16)
            d_copy(h).start()
            for k in range(SUPERS):
                for q in range(ANCESTORS):
                    tiles[k, q, :, h * HALF:(h + 1) * HALF] = -slot_tile(slots.at[h], k * ANCESTORS + q)

        half(0)
        gather2[1].finish()
        a_copy(1).start()
        half(1)
        diag_store.start()
        for k in range(SUPERS):
            out_copy(k, 0, ANCESTORS).start()
        for h in halves:
            a_copy(h).wait_send()
            d_copy(h).wait_send()
        for k in range(SUPERS):
            out_copy(k, 0, ANCESTORS).wait()
        diag_store.wait()

    @pl.when(layer == 1)
    def _():
        parents, places = [], []
        for k in range(SUPERS):
            parent = jnp.clip(anc[0, k, last] - TOP_BLOCKS, 0, SUPERS - 1)
            found = []
            for q in range(last):
                at = jnp.int32(0)
                for j in range(ANCESTORS):
                    at = jnp.where(anc_other[0, parent, j] == anc[0, k, q], j, at)
                found.append(parent * ANCESTORS + at)
            parents.append(parent)
            places.append(found)

        def turned_half(h):
            sums = []
            for k in range(SUPERS):
                total = jnp.zeros((BLOCK, HALF), F32)
                for q in range(last):
                    total += jnp.dot(
                        panel_t[k, q], slot_tile(sibling_slots[h], places[k][q]),
                        preferred_element_type=F32,
                    )
                sums.append(total.T)
            return sums

        a_copy(0).wait_recv()
        turned0 = turned_half(0)
        gather2[1].finish()
        a_copy(1).wait_recv()
        turned1 = turned_half(1)
        edges = [
            jnp.concatenate([panel_tile(h, k, last) for h in halves], axis=1) for k in range(SUPERS)
        ]
        for k in range(SUPERS):
            for q in range(last):
                whole = jnp.concatenate(
                    [slot_tile(sibling_slots[h], places[k][q]) for h in halves], axis=1
                )
                new = jnp.dot(whole, edges[k], preferred_element_type=F32)
                for h in halves:
                    old = slot_tile(slots.at[h], k * ANCESTORS + q).astype(F32)
                    tiles[k, q, :, h * HALF:(h + 1) * HALF] = (
                        new[:, h * HALF:(h + 1) * HALF] - old
                    ).astype(BF16)
            out_copy(k, 0, last).start()
        for h in halves:
            d_copy(h).wait_recv()
        for k in range(SUPERS):
            above = jnp.concatenate([sibling_diag[h, parents[k]] for h in halves], axis=1)
            turned = jnp.concatenate([turned0[k], turned1[k]], axis=0)
            tiles[k, last] = (
                turned - jnp.dot(above, edges[k], preferred_element_type=F32)
            ).astype(BF16)
            tiles[k, ANCESTORS] = (
                turned - jnp.dot(above.T, edges[k], preferred_element_type=F32)
            ).astype(BF16)
            out_copy(k, last, 2).start()
            total = dinv[0, k].astype(F32)
            for q in range(ANCESTORS):
                total -= jnp.dot(panel_t[k, q], tiles[k, q], preferred_element_type=F32)
            diag[0, k] = total.astype(BF16)
        diag_store.start()
        for k in range(SUPERS):
            out_copy(k, 0, last).wait()
            out_copy(k, last, 2).wait()
        diag_store.wait()

    anc_copy.wait_send()
    for h in halves:
        gather1[h].wait_sent()
        gather2[h].wait_sent()
        for copy in x_copies[h]:
            copy.wait_send()
        each_slot(h, lambda copy: copy.wait_send())


def place(anc, tiles, diag, col_out, row_out, diag_out, zero, col_sem, row_sem, diag_sem):
    layer = lax.axis_index("layer")
    x = lax.axis_index("prow")
    c = lax.axis_index("pcol")
    zero[...] = jnp.zeros_like(zero)
    diag_copy = pltpu.make_async_copy(diag, diag_out, diag_sem)
    diag_copy.start()

    def put(out, sems, first, blocks, row_side, start):
        for k in range(SUPERS):
            for j in range(blocks):
                dst = out.at[0, pl.ds(j * BLOCK, BLOCK), pl.ds(k * BLOCK, BLOCK)]
                sem = sems.at[k, j]
                if not start:
                    pltpu.make_async_copy(zero, dst, sem).wait()
                    continue
                at = jnp.int32(0)
                hit = jnp.int32(0)
                for q in range(ANCESTORS):
                    same = anc[0, k, q] == first + j
                    at = jnp.where(same, q, at)
                    hit = jnp.where(same, 1, hit)
                if row_side:
                    turned = jnp.logical_and(layer == 1, at == ANCESTORS - 1)
                    at = jnp.where(turned, ANCESTORS, at)

                @pl.when(hit > 0)
                def _():
                    pltpu.make_async_copy(tiles.at[k, at], dst, sem).start()

                @pl.when(hit == 0)
                def _():
                    pltpu.make_async_copy(zero, dst, sem).start()

    for start in (True, False):
        put(col_out, col_sem, x * ANCESTORS, ANCESTORS, False, start)
        put(row_out, row_sem, c * 2, 2, True, start)
    diag_copy.wait()


def body(stored_inverse, lhat, diag_inverse, ancestors):
    rows, cols = stored_inverse.shape
    stored = stored_inverse.reshape(rows // BLOCK, BLOCK, cols)
    anywhere = pl.BlockSpec(memory_space=pl.ANY)
    smem = pl.BlockSpec(memory_space=pltpu.SMEM)
    dma = pltpu.SemaphoreType.DMA
    width = SUPERS * BLOCK
    piece = (HALVES, SIDE, SIDE, SIDE, QUARTER, HALF)
    tiles, diag = pl.pallas_call(
        kernel,
        out_shape=(
            jax.ShapeDtypeStruct((SUPERS, ANCESTORS + 1, BLOCK, BLOCK), BF16),
            jax.ShapeDtypeStruct(diag_inverse.shape, BF16),
        ),
        in_specs=[anywhere] * 4,
        out_specs=(anywhere, anywhere),
        scratch_shapes=[
            pltpu.SMEM(ancestors.shape, jnp.int32),
            pltpu.VMEM(diag_inverse.shape, BF16),
            pltpu.VMEM(piece, BF16),
            pltpu.VMEM((rows // BLOCK, BLOCK, cols), BF16),
            pltpu.VMEM((SUPERS, ANCESTORS, SIDE, 2, QUARTER, BLOCK), BF16),
            pltpu.VMEM((SUPERS, ANCESTORS, BLOCK, BLOCK), BF16),
            pltpu.VMEM((HALVES, SIDE, SUPERS, 2, QUARTER, HALF), BF16),
            pltpu.VMEM((HALVES, SIDE - 1, SUPERS, 2, QUARTER, HALF), BF16),
            pltpu.VMEM((HALVES, SUPERS, 2, QUARTER, HALF), BF16),
            pltpu.VMEM((HALVES, SLOTS, QUARTER, HALF), BF16),
            pltpu.VMEM((PLANE, QUARTER, HALF), BF16),
            pltpu.VMEM((PLANE, QUARTER, HALF), BF16),
            pltpu.VMEM(piece, BF16),
            pltpu.VMEM(piece[1:], BF16),
            pltpu.VMEM(piece[1:], BF16),
            pltpu.VMEM((HALVES, SUPERS, BLOCK, HALF), BF16),
            pltpu.VMEM((HALVES, SUPERS, BLOCK, HALF), BF16),
            pltpu.VMEM((SUPERS, ANCESTORS + 1, BLOCK, BLOCK), BF16),
            pltpu.VMEM(diag_inverse.shape, BF16),
            pltpu.VMEM(ancestors.shape, jnp.int32),
            pltpu.SMEM(ancestors.shape, jnp.int32),
            dma, dma((4,)), dma, dma, dma,
            dma((HALVES, LINKS)), dma((HALVES, LINKS)), dma((HALVES, LINKS)), dma((HALVES, LINKS)),
            dma((HALVES, 3)), dma((HALVES, 3)), dma((HALVES, PLANE)), dma((HALVES, PLANE)),
            dma((HALVES,)), dma((HALVES,)), dma((HALVES,)), dma((HALVES,)), dma((3, 2)),
        ],
        compiler_params=pltpu.CompilerParams(
            collective_id=0, has_side_effects=True, vmem_limit_bytes=VMEM_LIMIT
        ),
        name="selected_inverse",
    )(ancestors, lhat, stored, diag_inverse)
    return pl.pallas_call(
        place,
        out_shape=(
            jax.ShapeDtypeStruct((1, rows, width), BF16),
            jax.ShapeDtypeStruct((1, cols, width), BF16),
            jax.ShapeDtypeStruct(diag_inverse.shape, BF16),
        ),
        in_specs=[smem, anywhere, anywhere],
        out_specs=(anywhere, anywhere, anywhere),
        scratch_shapes=[
            pltpu.VMEM((BLOCK, BLOCK), BF16),
            dma((SUPERS, ANCESTORS)), dma((SUPERS, 2)), dma,
        ],
        compiler_params=pltpu.CompilerParams(vmem_limit_bytes=VMEM_LIMIT),
        name="placed_tiles",
    )(ancestors, tiles, diag)


def solution(mesh):
    return jax.shard_map(
        body,
        mesh=mesh,
        in_specs=(
            P("prow", "pcol"),
            P("layer", ("prow", "pcol"), None),
            P("layer", None, None, None),
            P("layer", None, None),
        ),
        out_specs=(
            P("layer", "prow", None),
            P("layer", "pcol", None),
            P("layer", None, None, None),
        ),
        check_vma=False,
    )
```

```python
import functools

import jax
import jax.numpy as jnp
from jax import lax
from jax.experimental import pallas as pl
from jax.experimental.pallas import tpu as pltpu
from jax.sharding import PartitionSpec as P

BLOCK = 256
ANCESTORS = 8
SUPERS = 2
TOP_BLOCKS = 28
SIDE = 4
PLANE = 16
QUARTER = 64
HALVES = 2
HALF = BLOCK // HALVES
SLOTS = SUPERS * ANCESTORS
MESH = pl.DeviceIdType.MESH
BF16 = jnp.bfloat16
F32 = jnp.float32
VMEM_LIMIT = 60 << 20

ROUTES = (
    ((("y", "z", "x"), 0, 32), (("x", "z", "y"), 32, 32)),
    ((("y", "z", "x"), 0, 16), (("z", "x", "y"), 16, 16), (("x", "y", "z"), 32, 32)),
)
HOPS = (2, 1, 3)
LINKS = 56


class Gather:
    def __init__(self, buf, dims, me, layer, routes, send, recv):
        self.buf, self.dims, self.me, self.layer, self.routes = buf, dims, me, layer, routes
        self.send, self.recv = send, recv
        self.count = 0
        self.sent, self.second, self.third = [], [], []

    def copies(self, route, full, axis, fixed=None):
        _, first, rows = route
        fixed = fixed or {}
        index = tuple(
            fixed[d] if d in fixed else pl.ds(0, SIDE) if d in full else self.me[d]
            for d in self.dims
        )
        part = self.buf.at[index + (pl.ds(first, rows),)]
        made = []
        for hop in HOPS:
            at = dict(self.me)
            at[axis] = (self.me[axis] + hop) % SIDE
            copy = pltpu.make_async_remote_copy(
                src_ref=part, dst_ref=part,
                send_sem=self.send.at[self.count], recv_sem=self.recv.at[self.count],
                device_id=(self.layer, at["x"], at["z"] * SIDE + at["y"]), device_id_type=MESH,
            )
            self.count += 1
            copy.start()
            made.append(copy)
        self.sent += made
        return made

    def start(self):
        self.first = [self.copies(route, (), route[0][0]) for route in self.routes]

    def after_first(self):
        for route, arriving in zip(self.routes, self.first):
            order = route[0]
            for copy in arriving:
                copy.wait_recv()
            self.second.append(self.copies(route, order[:1], order[1]))
        for route in self.routes:
            order = route[0]
            self.third += self.copies(route, order[:1], order[2])

    def after_second(self):
        for n, hop in enumerate(HOPS):
            for route, arriving in zip(self.routes, self.second):
                order = route[0]
                arriving[n].wait_recv()
                came_from = (self.me[order[1]] + SIDE - hop) % SIDE
                self.third += self.copies(route, order[:1], order[2], {order[1]: came_from})

    def finish(self):
        for copy in self.third:
            copy.wait_recv()

    def wait_sent(self):
        for copy in self.sent:
            copy.wait_send()


def kernel(
    anc_any, panel_any, g_any, dinv_any,
    tiles_out, diag_out,
    anc, dinv, panels, g_own, g_pick, panel_t, partial, partial_in, summed, staged, moved0, moved1, slots,
    sibling_slots0, sibling_slots1, sibling_diag, diag_send, tiles, diag, anc_in, anc_other,
    g_sem, in_sem, anc_send, anc_recv, anc_local,
    send1, recv1, send2, recv2, x_send, x_recv, c_send, c_recv, a_send, a_recv, d_send, d_recv, out_sem,
):
    layer = lax.axis_index("layer")
    x = lax.axis_index("prow")
    c = lax.axis_index("pcol")
    z = c // SIDE
    y = c % SIDE
    me = {"x": x, "y": y, "z": z}
    halves = range(HALVES)
    last = ANCESTORS - 1
    moved = (moved0, moved1)
    sibling_slots = (sibling_slots0, sibling_slots1)

    in_copies = [
        pltpu.make_async_copy(
            panel_any.at[0, :, pl.ds(h * HALF, HALF)], panels.at[h, x, z, y], in_sem.at[h]
        )
        for h in halves
    ]
    anc_load = pltpu.make_async_copy(anc_any, anc, in_sem.at[2])
    dinv_load = pltpu.make_async_copy(dinv_any, dinv, in_sem.at[3])
    g_load = pltpu.make_async_copy(g_any, g_own, g_sem)
    for copy in in_copies:
        copy.start()
    anc_load.start()
    g_load.start()
    dinv_load.start()

    barrier = pltpu.get_barrier_semaphore()

    def greet_plane(step, carry):
        pl.semaphore_signal(barrier, inc=1, device_id=(layer, x, (c + step) % PLANE), device_id_type=MESH)
        return carry

    def greet_line(step, carry):
        pl.semaphore_signal(barrier, inc=1, device_id=(layer, (x + step) % SIDE, c), device_id_type=MESH)
        return carry

    lax.fori_loop(1, PLANE, greet_plane, 0)
    lax.fori_loop(1, SIDE, greet_line, 0)
    pl.semaphore_signal(barrier, inc=1, device_id=(1 - layer, x, c), device_id_type=MESH)
    pl.semaphore_wait(barrier, PLANE - 1 + SIDE - 1 + 1)

    gather1 = [
        Gather(panels.at[h], ("x", "z", "y"), me, layer, ROUTES[h], send1.at[h], recv1.at[h])
        for h in halves
    ]
    gather2 = [
        Gather(slots.at[h], ("z", "y", "x"), me, layer, ROUTES[h], send2.at[h], recv2.at[h])
        for h in halves
    ]
    for copy in in_copies:
        copy.wait()
    gather1[0].start()
    sibling = (1 - layer, x, c)
    anc_copy = pltpu.make_async_remote_copy(
        src_ref=anc_any, dst_ref=anc_in, send_sem=anc_send, recv_sem=anc_recv,
        device_id=sibling, device_id_type=MESH,
    )
    anc_copy.start()
    anc_load.wait()
    g_load.wait()
    dinv_load.wait()

    def pick_blocks(k):
        def pick(p, carry):
            at = anc[0, k, p] - x * ANCESTORS
            here = jnp.logical_and(at >= 0, at < ANCESTORS)
            block = g_own[jnp.clip(at, 0, ANCESTORS - 1)]
            block = jnp.where(here, block, jnp.zeros_like(block))
            turned = block.T
            for b in range(2):
                for q in range(SIDE):
                    first = b * BLOCK + q * QUARTER
                    g_pick[k, p, q, b] = turned[first:first + QUARTER]
            return carry
        lax.fori_loop(0, ANCESTORS, pick, 0)

    def panel_tile(h, k, p):
        return panels[h, 2 * k + p // SIDE, p % SIDE].reshape(BLOCK, HALF)

    def multiply(h):
        for k in range(SUPERS):
            total = jnp.zeros((2 * BLOCK, HALF), F32)
            for p in range(ANCESTORS):
                total += jnp.dot(
                    g_pick[k, p].reshape(2 * BLOCK, BLOCK), panel_tile(h, k, p),
                    preferred_element_type=F32,
                )
            partial[h, :, k] = total.astype(BF16).reshape(SIDE, 2, QUARTER, HALF)

    x_copies = [[], []]

    def start_reduce(h):
        for hop in HOPS:
            to = (x + hop) % SIDE
            copy = pltpu.make_async_remote_copy(
                src_ref=partial.at[h, to], dst_ref=partial_in.at[h, hop - 1],
                send_sem=x_send.at[h, hop - 1], recv_sem=x_recv.at[h, hop - 1],
                device_id=(layer, to, c), device_id_type=MESH,
            )
            copy.start()
            x_copies[h].append(copy)

    def turn_panels(h):
        for k in range(SUPERS):
            for p in range(ANCESTORS):
                panel_t[k, p, h * HALF:(h + 1) * HALF, :] = panel_tile(h, k, p).T

    def to_slot(h, step):
        to = (c + step) % PLANE
        return pltpu.make_async_remote_copy(
            src_ref=staged.at[h, to], dst_ref=moved[h].at[c],
            send_sem=c_send.at[h, step], recv_sem=c_recv.at[h, step],
            device_id=(layer, x, to), device_id_type=MESH,
        )

    def each_slot(h, act):
        def step_of(step, carry):
            act(to_slot(h, step))
            return carry
        lax.fori_loop(1, PLANE, step_of, 0)

    def start_move(h):
        for copy in x_copies[h]:
            copy.wait_recv()
        total = partial[h, x].astype(F32)
        for hop in HOPS:
            total += partial_in[h, hop - 1].astype(F32)
        summed[h] = total.astype(BF16)
        for s in range(SLOTS):
            at = jnp.clip(anc[0, s // ANCESTORS, s % ANCESTORS] - 2 * c, 0, 1)
            staged[h, s] = summed[h, s // ANCESTORS, at]
        each_slot(h, lambda copy: copy.start())
        moved[h][c] = staged[h, c]

    def end_move(h):
        each_slot(h, lambda copy: copy.wait_recv())
        holder = anc[0, c // ANCESTORS, c % ANCESTORS] // 2
        slots[h, z, y, x] = moved[h][holder]

    def a_copy(h):
        return pltpu.make_async_remote_copy(
            src_ref=slots.at[h], dst_ref=sibling_slots[h], send_sem=a_send.at[h], recv_sem=a_recv.at[h],
            device_id=sibling, device_id_type=MESH,
        )

    def d_copy(h):
        return pltpu.make_async_remote_copy(
            src_ref=diag_send.at[h], dst_ref=sibling_diag.at[h], send_sem=d_send.at[h], recv_sem=d_recv.at[h],
            device_id=sibling, device_id_type=MESH,
        )

    def slot_tile(ref, s):
        return ref[s // SIDE, s % SIDE].reshape(BLOCK, HALF)

    def out_copy(k, first, count):
        return pltpu.make_async_copy(
            tiles.at[k, pl.ds(first, count)], tiles_out.at[k, pl.ds(first, count)],
            out_sem.at[k, first // last],
        )

    diag_store = pltpu.make_async_copy(diag, diag_out, out_sem.at[2, 0])

    pick_blocks(0)
    gather1[0].after_first()
    gather1[1].start()
    pick_blocks(1)
    gather1[0].after_second()
    gather1[1].after_first()
    gather1[0].finish()
    gather1[1].after_second()
    multiply(0)
    start_reduce(0)
    turn_panels(0)
    gather1[1].finish()
    multiply(1)
    start_reduce(1)
    start_move(0)
    turn_panels(1)
    start_move(1)
    end_move(0)
    gather2[0].start()
    anc_copy.wait_recv()
    to_smem = pltpu.make_async_copy(anc_in, anc_other, anc_local)
    to_smem.start()
    to_smem.wait()
    gather2[0].after_first()
    end_move(1)
    gather2[1].start()
    gather2[0].after_second()
    gather2[1].after_first()
    gather2[0].finish()

    @pl.when(layer == 0)
    def _():
        a_copy(0).start()

    gather2[1].after_second()

    @pl.when(layer == 0)
    def _():
        def half(h):
            for k in range(SUPERS):
                total = dinv[0, k, :, h * HALF:(h + 1) * HALF].astype(F32)
                for q in range(ANCESTORS):
                    total += jnp.dot(
                        panel_t[k, q], slot_tile(slots.at[h], k * ANCESTORS + q),
                        preferred_element_type=F32,
                    )
                diag_send[h, k] = total.astype(BF16)
                diag[0, k, :, h * HALF:(h + 1) * HALF] = total.astype(BF16)
            d_copy(h).start()
            for k in range(SUPERS):
                for q in range(ANCESTORS):
                    tiles[k, q, :, h * HALF:(h + 1) * HALF] = -slot_tile(slots.at[h], k * ANCESTORS + q)

        half(0)
        gather2[1].finish()
        a_copy(1).start()
        half(1)
        diag_store.start()
        for k in range(SUPERS):
            out_copy(k, 0, ANCESTORS).start()
        for h in halves:
            a_copy(h).wait_send()
            d_copy(h).wait_send()
        for k in range(SUPERS):
            out_copy(k, 0, ANCESTORS).wait()
        diag_store.wait()

    @pl.when(layer == 1)
    def _():
        parents, places = [], []
        for k in range(SUPERS):
            parent = jnp.clip(anc[0, k, last] - TOP_BLOCKS, 0, SUPERS - 1)
            found = []
            for q in range(last):
                at = jnp.int32(0)
                for j in range(ANCESTORS):
                    at = jnp.where(anc_other[0, parent, j] == anc[0, k, q], j, at)
                found.append(parent * ANCESTORS + at)
            parents.append(parent)
            places.append(found)

        def turned_half(h):
            sums = []
            for k in range(SUPERS):
                total = jnp.zeros((BLOCK, HALF), F32)
                for q in range(last):
                    total += jnp.dot(
                        panel_t[k, q], slot_tile(sibling_slots[h], places[k][q]),
                        preferred_element_type=F32,
                    )
                sums.append(total.T)
            return sums

        a_copy(0).wait_recv()
        turned0 = turned_half(0)
        gather2[1].finish()
        a_copy(1).wait_recv()
        turned1 = turned_half(1)
        edges = [
            jnp.concatenate([panel_tile(h, k, last) for h in halves], axis=1) for k in range(SUPERS)
        ]
        for k in range(SUPERS):
            for q in range(last):
                whole = jnp.concatenate(
                    [slot_tile(sibling_slots[h], places[k][q]) for h in halves], axis=1
                )
                new = jnp.dot(whole, edges[k], preferred_element_type=F32)
                for h in halves:
                    old = slot_tile(slots.at[h], k * ANCESTORS + q).astype(F32)
                    tiles[k, q, :, h * HALF:(h + 1) * HALF] = (
                        new[:, h * HALF:(h + 1) * HALF] - old
                    ).astype(BF16)
            out_copy(k, 0, last).start()
        for h in halves:
            d_copy(h).wait_recv()
        for k in range(SUPERS):
            above = jnp.concatenate([sibling_diag[h, parents[k]] for h in halves], axis=1)
            turned = jnp.concatenate([turned0[k], turned1[k]], axis=0)
            tiles[k, last] = (
                turned - jnp.dot(above, edges[k], preferred_element_type=F32)
            ).astype(BF16)
            tiles[k, ANCESTORS] = (
                turned - jnp.dot(above.T, edges[k], preferred_element_type=F32)
            ).astype(BF16)
            out_copy(k, last, 2).start()
            total = dinv[0, k].astype(F32)
            for q in range(ANCESTORS):
                total -= jnp.dot(panel_t[k, q], tiles[k, q], preferred_element_type=F32)
            diag[0, k] = total.astype(BF16)
        diag_store.start()
        for k in range(SUPERS):
            out_copy(k, 0, last).wait()
            out_copy(k, last, 2).wait()
        diag_store.wait()

    anc_copy.wait_send()
    for h in halves:
        gather1[h].wait_sent()
        gather2[h].wait_sent()
        for copy in x_copies[h]:
            copy.wait_send()
        each_slot(h, lambda copy: copy.wait_send())


def place(anc, tiles, diag, col_out, row_out, diag_out, zero, col_sem, row_sem, diag_sem):
    layer = lax.axis_index("layer")
    x = lax.axis_index("prow")
    c = lax.axis_index("pcol")
    zero[...] = jnp.zeros_like(zero)
    diag_copy = pltpu.make_async_copy(diag, diag_out, diag_sem)
    diag_copy.start()

    def put(out, sems, first, blocks, row_side, start):
        for k in range(SUPERS):
            for j in range(blocks):
                dst = out.at[0, pl.ds(j * BLOCK, BLOCK), pl.ds(k * BLOCK, BLOCK)]
                sem = sems.at[k, j]
                if not start:
                    pltpu.make_async_copy(zero, dst, sem).wait()
                    continue
                at = jnp.int32(0)
                hit = jnp.int32(0)
                for q in range(ANCESTORS):
                    same = anc[0, k, q] == first + j
                    at = jnp.where(same, q, at)
                    hit = jnp.where(same, 1, hit)
                if row_side:
                    turned = jnp.logical_and(layer == 1, at == ANCESTORS - 1)
                    at = jnp.where(turned, ANCESTORS, at)

                @pl.when(hit > 0)
                def _():
                    pltpu.make_async_copy(tiles.at[k, at], dst, sem).start()

                @pl.when(hit == 0)
                def _():
                    pltpu.make_async_copy(zero, dst, sem).start()

    for start in (True, False):
        put(col_out, col_sem, x * ANCESTORS, ANCESTORS, False, start)
        put(row_out, row_sem, c * 2, 2, True, start)
    diag_copy.wait()


def body(stored_inverse, lhat, diag_inverse, ancestors):
    rows, cols = stored_inverse.shape
    stored = stored_inverse.reshape(rows // BLOCK, BLOCK, cols)
    anywhere = pl.BlockSpec(memory_space=pl.ANY)
    vmem = pl.BlockSpec(memory_space=pltpu.VMEM)
    smem = pl.BlockSpec(memory_space=pltpu.SMEM)
    dma = pltpu.SemaphoreType.DMA
    width = SUPERS * BLOCK
    piece = (HALVES, SIDE, SIDE, SIDE, QUARTER, HALF)
    tiles, diag = pl.pallas_call(
        kernel,
        out_shape=(
            pltpu.VMEM((SUPERS, ANCESTORS + 1, BLOCK, BLOCK), BF16),
            pltpu.VMEM(diag_inverse.shape, BF16),
        ),
        in_specs=[anywhere] * 4,
        out_specs=(vmem, vmem),
        scratch_shapes=[
            pltpu.SMEM(ancestors.shape, jnp.int32),
            pltpu.VMEM(diag_inverse.shape, BF16),
            pltpu.VMEM(piece, BF16),
            pltpu.VMEM((rows // BLOCK, BLOCK, cols), BF16),
            pltpu.VMEM((SUPERS, ANCESTORS, SIDE, 2, QUARTER, BLOCK), BF16),
            pltpu.VMEM((SUPERS, ANCESTORS, BLOCK, BLOCK), BF16),
            pltpu.VMEM((HALVES, SIDE, SUPERS, 2, QUARTER, HALF), BF16),
            pltpu.VMEM((HALVES, SIDE - 1, SUPERS, 2, QUARTER, HALF), BF16),
            pltpu.VMEM((HALVES, SUPERS, 2, QUARTER, HALF), BF16),
            pltpu.VMEM((HALVES, SLOTS, QUARTER, HALF), BF16),
            pltpu.VMEM((PLANE, QUARTER, HALF), BF16),
            pltpu.VMEM((PLANE, QUARTER, HALF), BF16),
            pltpu.VMEM(piece, BF16),
            pltpu.VMEM(piece[1:], BF16),
            pltpu.VMEM(piece[1:], BF16),
            pltpu.VMEM((HALVES, SUPERS, BLOCK, HALF), BF16),
            pltpu.VMEM((HALVES, SUPERS, BLOCK, HALF), BF16),
            pltpu.VMEM((SUPERS, ANCESTORS + 1, BLOCK, BLOCK), BF16),
            pltpu.VMEM(diag_inverse.shape, BF16),
            pltpu.VMEM(ancestors.shape, jnp.int32),
            pltpu.SMEM(ancestors.shape, jnp.int32),
            dma, dma((4,)), dma, dma, dma,
            dma((HALVES, LINKS)), dma((HALVES, LINKS)), dma((HALVES, LINKS)), dma((HALVES, LINKS)),
            dma((HALVES, 3)), dma((HALVES, 3)), dma((HALVES, PLANE)), dma((HALVES, PLANE)),
            dma((HALVES,)), dma((HALVES,)), dma((HALVES,)), dma((HALVES,)), dma((3, 2)),
        ],
        compiler_params=pltpu.CompilerParams(
            collective_id=0, has_side_effects=True, vmem_limit_bytes=VMEM_LIMIT
        ),
        name="selected_inverse",
    )(ancestors, lhat, stored, diag_inverse)
    return pl.pallas_call(
        place,
        out_shape=(
            jax.ShapeDtypeStruct((1, rows, width), BF16),
            jax.ShapeDtypeStruct((1, cols, width), BF16),
            jax.ShapeDtypeStruct(diag_inverse.shape, BF16),
        ),
        in_specs=[smem, vmem, vmem],
        out_specs=(anywhere, anywhere, anywhere),
        scratch_shapes=[
            pltpu.VMEM((BLOCK, BLOCK), BF16),
            dma((SUPERS, ANCESTORS)), dma((SUPERS, 2)), dma,
        ],
        compiler_params=pltpu.CompilerParams(vmem_limit_bytes=VMEM_LIMIT // 8),
        name="placed_tiles",
    )(ancestors, tiles, diag)


def solution(mesh):
    return jax.shard_map(
        body,
        mesh=mesh,
        in_specs=(
            P("prow", "pcol"),
            P("layer", ("prow", "pcol"), None),
            P("layer", None, None, None),
            P("layer", None, None),
        ),
        out_specs=(
            P("layer", "prow", None),
            P("layer", "pcol", None),
            P("layer", None, None, None),
        ),
        check_vma=False,
    )
```

```python
import jax
import jax.numpy as jnp
from jax import lax
from jax.experimental import pallas as pl
from jax.experimental.pallas import tpu as pltpu
from jax.sharding import PartitionSpec as P

BLOCK = 256
ANCESTORS = 8
SUPERS = 2
TOP_BLOCKS = 28
SIDE = 4
PLANE = 16
PIECES = 64
QUARTER = 64
SLOTS = SUPERS * ANCESTORS
LAST = ANCESTORS - 1
MESH = pl.DeviceIdType.MESH
BF16 = jnp.bfloat16
F32 = jnp.float32
VMEM_LIMIT = 60 << 20

ROUTES = (
    (("y", "z", "x"), (0, 48), (0, 128)),
    (("x", "z", "y"), (0, 48), (128, 128)),
    (("x", "y", "z"), (48, 16), (0, 256)),
)
HOPS = (2, 1, 3)
ARRIVALS = (1, 3, 2)
UNIT = 16 * 128
PIECE = QUARTER * BLOCK // UNIT


def units(route):
    return route[1][1] * route[2][1] // UNIT


class Gather:
    def __init__(self, buf, dims, me, layer, wait, send, first, second, third):
        self.buf, self.dims, self.me, self.layer, self.wait = buf, dims, me, layer, wait
        self.send, self.first, self.second, self.third = send, first, second, third

    def part(self, route, full, fixed=None):
        fixed = fixed or {}
        index = tuple(
            fixed[d] if d in fixed else pl.ds(0, SIDE) if d in full else self.me[d]
            for d in self.dims
        )
        return index + (pl.ds(*route[1]), pl.ds(*route[2]))

    def copies(self, route, full, axis, sem_of, fixed=None):
        part = self.buf.at[self.part(route, full, fixed)]
        for hop in HOPS:
            at = dict(self.me)
            at[axis] = (self.me[axis] + hop) % SIDE
            pltpu.make_async_remote_copy(
                src_ref=part, dst_ref=part, send_sem=self.send, recv_sem=sem_of(hop),
                device_id=(self.layer, at["x"], at["z"] * SIDE + at["y"]), device_id_type=MESH,
            ).start()

    def start(self):
        for r, route in enumerate(ROUTES):
            self.copies(route, (), route[0][0], lambda hop: self.first.at[r])

    def after_first(self):
        for r, route in enumerate(ROUTES):
            order = route[0]
            self.wait(self.first.at[r], 3 * units(route))
            self.copies(route, order[:1], order[1], lambda hop: self.second.at[r, hop - 1])
        for r, route in enumerate(ROUTES):
            order = route[0]
            self.copies(route, order[:1], order[2], lambda hop: self.third.at[r, hop - 1])

    def after_second(self):
        for hop in ARRIVALS:
            for r, route in enumerate(ROUTES):
                order = route[0]
                self.wait(self.second.at[r, hop - 1], SIDE * units(route))
                came_from = (self.me[order[1]] + SIDE - hop) % SIDE
                self.copies(
                    route, order[:1], order[2], lambda to: self.third.at[r, to - 1], {order[1]: came_from}
                )

    def own_planes(self, act):
        for route in ROUTES:
            act(self.part(route, route[0][:2]))

    def finish(self, act=None):
        for hop in ARRIVALS:
            for r, route in enumerate(ROUTES):
                order = route[0]
                self.wait(self.third.at[r, hop - 1], PLANE * units(route))
                if act is not None:
                    came_from = (self.me[order[2]] + SIDE - hop) % SIDE
                    act(self.part(route, order[:2], {order[2]: came_from}))

    def wait_sent(self):
        self.wait(self.send, (PIECES - 1) * PIECE)


def kernel(
    anc_any, panel_any, g_any, dinv_any,
    tiles, diag,
    anc, dinv, panels, g_own, g_pick, panel_t, partial, partial_in, summed, staged, moved, slots,
    other_slots, other_panel_t, other_edges, diag_now, corner_send, corner_in, anc_in, anc_other, measure,
    in_sem, anc_sem,
    send1, first1, second1, third1, send2, first2, second2, third2,
    x_send, x_recv, c_send, c_recv, a_send, a_recv, m_send, m_recv, e_send, e_recv,
):
    layer = lax.axis_index("layer")
    x = lax.axis_index("prow")
    c = lax.axis_index("pcol")
    z = c // SIDE
    y = c % SIDE
    me = {"x": x, "y": y, "z": z}
    sibling = (1 - layer, x, c)

    def wait(sem, count):
        ref = measure.at[pl.ds(0, count)]
        pltpu.make_async_copy(ref, ref, sem).wait()

    def to_sibling(src, dst, send, recv):
        return pltpu.make_async_remote_copy(
            src_ref=src, dst_ref=dst, send_sem=send, recv_sem=recv, device_id=sibling, device_id_type=MESH
        )

    panel_load = pltpu.make_async_copy(panel_any, panels.at[x, z, pl.ds(y, 1)], in_sem.at[0])
    anc_load = pltpu.make_async_copy(anc_any, anc, in_sem.at[1])
    dinv_load = pltpu.make_async_copy(dinv_any, dinv, in_sem.at[2])
    g_load = pltpu.make_async_copy(g_any, g_own, in_sem.at[3])
    panel_load.start()
    anc_load.start()
    g_load.start()
    dinv_load.start()

    barrier = pltpu.get_barrier_semaphore()

    def greet_plane(step, carry):
        pl.semaphore_signal(barrier, inc=1, device_id=(layer, x, (c + step) % PLANE), device_id_type=MESH)
        return carry

    def greet_line(step, carry):
        pl.semaphore_signal(barrier, inc=1, device_id=(layer, (x + step) % SIDE, c), device_id_type=MESH)
        return carry

    lax.fori_loop(1, PLANE, greet_plane, 0)
    lax.fori_loop(1, SIDE, greet_line, 0)
    pl.semaphore_signal(barrier, inc=1, device_id=sibling, device_id_type=MESH)
    pl.semaphore_wait(barrier, PLANE - 1 + SIDE - 1 + 1)

    gather1 = Gather(panels, ("x", "z", "y"), me, layer, wait, send1, first1, second1, third1)
    gather2 = Gather(slots, ("z", "y", "x"), me, layer, wait, send2, first2, second2, third2)
    panel_load.wait()
    gather1.start()
    anc_copy = to_sibling(anc_any, anc_in, anc_sem.at[0], anc_sem.at[1])
    anc_copy.start()
    anc_load.wait()
    dinv_load.wait()
    g_load.wait()

    def pick_blocks(k):
        def pick(p, carry):
            at = anc[0, k, p] - x * ANCESTORS
            here = jnp.logical_and(at >= 0, at < ANCESTORS)
            block = g_own[jnp.clip(at, 0, ANCESTORS - 1)]
            block = jnp.where(here, block, jnp.zeros_like(block))
            turned = block.T
            for b in range(2):
                for q in range(SIDE):
                    first = b * BLOCK + q * QUARTER
                    g_pick[k, p, q, b] = turned[first:first + QUARTER]
            return carry
        lax.fori_loop(0, ANCESTORS, pick, 0)

    def tile_of(ref, s):
        return ref[s // SIDE, s % SIDE].reshape(BLOCK, BLOCK)

    def multiply(k):
        total = jnp.zeros((2 * BLOCK, BLOCK), F32)
        for p in range(ANCESTORS):
            total += jnp.dot(
                g_pick[k, p].reshape(2 * BLOCK, BLOCK), tile_of(panels, k * ANCESTORS + p),
                preferred_element_type=F32,
            )
        partial[k] = total.astype(BF16).reshape(SIDE, 2, QUARTER, BLOCK)

    def start_reduce(k):
        for hop in HOPS:
            to = (x + hop) % SIDE
            pltpu.make_async_remote_copy(
                src_ref=partial.at[k, to], dst_ref=partial_in.at[k, hop - 1],
                send_sem=x_send, recv_sem=x_recv.at[k],
                device_id=(layer, to, c), device_id_type=MESH,
            ).start()

    def turn_panels():
        for k in range(SUPERS):
            def turn(p, carry):
                s = k * ANCESTORS + p
                panel_t[k, p] = tile_of(panels, s).T
                return carry
            lax.fori_loop(0, ANCESTORS, turn, 0)

    def start_move(k):
        wait(x_recv.at[k], 3 * 2 * PIECE)
        total = partial[k, x].astype(F32)
        for hop in HOPS:
            total += partial_in[k, hop - 1].astype(F32)
        summed[k] = total.astype(BF16)
        for q in range(ANCESTORS):
            staged[k * ANCESTORS + q] = summed[k, jnp.clip(anc[0, k, q] - 2 * c, 0, 1)]

        def send(step, carry):
            to = k * ANCESTORS + (c + step) % ANCESTORS

            @pl.when(to != c)
            def _():
                pltpu.make_async_remote_copy(
                    src_ref=staged.at[to], dst_ref=moved.at[c], send_sem=c_send, recv_sem=c_recv,
                    device_id=(layer, x, to), device_id_type=MESH,
                ).start()
            return carry
        lax.fori_loop(0, ANCESTORS, send, 0)

    def end_move():
        moved[c] = staged[c]
        wait(c_recv, (PLANE - 1) * PIECE)
        holder = anc[0, c // ANCESTORS, c % ANCESTORS] // 2
        slots[z, y, x] = moved[holder]

    gather1.after_first()
    pick_blocks(0)
    gather1.after_second()
    pick_blocks(1)
    gather1.finish()
    multiply(0)
    start_reduce(0)
    multiply(1)
    start_reduce(1)
    turn_panels()

    @pl.when(layer == 1)
    def _():
        to_sibling(panel_t, other_panel_t, m_send.at[0], m_recv.at[0]).start()
        for k in range(SUPERS):
            to_sibling(
                panels.at[2 * k + 1, SIDE - 1], other_edges.at[k], m_send.at[k + 1], m_recv.at[k + 1]
            ).start()

    anc_copy.wait_recv()
    to_smem = pltpu.make_async_copy(anc_in, anc_other, in_sem.at[1])
    to_smem.start()
    to_smem.wait()
    start_move(0)
    start_move(1)
    end_move()
    gather2.start()

    def find_parents(above, below):
        parents, places = [], []
        for k in range(SUPERS):
            parent = jnp.clip(below[0, k, LAST] - TOP_BLOCKS, 0, SUPERS - 1)
            found = []
            for q in range(LAST):
                at = jnp.int32(0)
                for j in range(ANCESTORS):
                    at = jnp.where(above[0, parent, j] == below[0, k, q], j, at)
                found.append(parent * ANCESTORS + at)
            parents.append(parent)
            places.append(found)
        return parents, places

    gather2.after_first()
    gather2.after_second()

    def pass_on(part):
        to_sibling(slots.at[part], other_slots.at[part], a_send, a_recv).start()

    def corner_copy(k):
        return to_sibling(corner_send.at[k], corner_in.at[k], e_send.at[k], e_recv.at[k])

    def matrix(a, b):
        return jnp.dot(a, b, preferred_element_type=F32)

    @pl.when(layer == 0)
    def _():
        parents, places = find_parents(anc, anc_other)
        gather2.own_planes(pass_on)
        gather2.finish(pass_on)
        to_sibling(panel_t, other_panel_t, m_send.at[0], m_recv.at[0]).wait_recv()
        for k in range(SUPERS):
            to_sibling(
                panels.at[2 * k + 1, SIDE - 1], other_edges.at[k], m_send.at[k + 1], m_recv.at[k + 1]
            ).wait_recv()
        for k in range(SUPERS):
            total = dinv[0, k].astype(F32)
            for q in range(ANCESTORS):
                total += matrix(panel_t[k, q], tile_of(slots, k * ANCESTORS + q))
            diag[0, k] = total.astype(BF16)
            diag_now[k] = total.astype(BF16)
        for k in range(SUPERS):
            total = jnp.zeros((BLOCK, BLOCK), F32)
            for q in range(LAST):
                total += matrix(other_panel_t[k, q], tile_of(slots, places[k][q]))
            above = diag_now[parents[k]]
            edge = other_edges[k].reshape(BLOCK, BLOCK)
            turned = total.T
            corner_send[k, 0] = (turned - matrix(above, edge)).astype(BF16)
            corner_send[k, 1] = (turned - matrix(above.T, edge)).astype(BF16)
            corner_send[k, 2] = total.astype(BF16)
            corner_copy(k).start()
        for k in range(SUPERS):
            for q in range(ANCESTORS):
                tiles[k, q] = -tile_of(slots, k * ANCESTORS + q)
        wait(a_send, PIECES * PIECE)
        for k in range(SUPERS):
            corner_copy(k).wait_send()

    @pl.when(layer == 1)
    def _():
        parents, places = find_parents(anc_other, anc)
        gather2.finish()
        sums = []
        for k in range(SUPERS):
            total = dinv[0, k].astype(F32)
            for q in range(LAST):
                total += matrix(panel_t[k, q], tile_of(slots, k * ANCESTORS + q))
            sums.append(total)
        wait(a_recv, PIECES * PIECE)
        for k in range(SUPERS):
            edge = tile_of(panels, k * ANCESTORS + LAST)
            for q in range(LAST):
                new = matrix(tile_of(other_slots, places[k][q]), edge)
                tiles[k, q] = (new - tile_of(slots, k * ANCESTORS + q).astype(F32)).astype(BF16)
        for k in range(SUPERS):
            corner_copy(k).wait_recv()
            corner = corner_in[k, 0]
            tiles[k, LAST] = corner
            tiles[k, ANCESTORS] = corner_in[k, 1]
            edge = tile_of(panels, k * ANCESTORS + LAST)
            total = sums[k] - matrix(corner_in[k, 2], edge) - matrix(panel_t[k, LAST], corner)
            diag[0, k] = total.astype(BF16)
        to_sibling(panel_t, other_panel_t, m_send.at[0], m_recv.at[0]).wait_send()
        for k in range(SUPERS):
            to_sibling(
                panels.at[2 * k + 1, SIDE - 1], other_edges.at[k], m_send.at[k + 1], m_recv.at[k + 1]
            ).wait_send()

    anc_copy.wait_send()
    gather1.wait_sent()
    gather2.wait_sent()
    wait(x_send, SUPERS * 3 * 2 * PIECE)
    wait(c_send, (PLANE - 1) * PIECE)


def place(anc, tiles, diag, col_out, row_out, diag_out, zero, col_sem, row_sem, diag_sem):
    layer = lax.axis_index("layer")
    x = lax.axis_index("prow")
    c = lax.axis_index("pcol")
    zero[...] = jnp.zeros_like(zero)
    diag_copy = pltpu.make_async_copy(diag, diag_out, diag_sem)
    diag_copy.start()

    def put(out, sems, first, blocks, row_side, start):
        for k in range(SUPERS):
            for j in range(blocks):
                dst = out.at[0, pl.ds(j * BLOCK, BLOCK), pl.ds(k * BLOCK, BLOCK)]
                sem = sems.at[k, j]
                if not start:
                    pltpu.make_async_copy(zero, dst, sem).wait()
                    continue
                at = jnp.int32(0)
                hit = jnp.int32(0)
                for q in range(ANCESTORS):
                    same = anc[0, k, q] == first + j
                    at = jnp.where(same, q, at)
                    hit = jnp.where(same, 1, hit)
                if row_side:
                    turned = jnp.logical_and(layer == 1, at == ANCESTORS - 1)
                    at = jnp.where(turned, ANCESTORS, at)

                @pl.when(hit > 0)
                def _():
                    pltpu.make_async_copy(tiles.at[k, at], dst, sem).start()

                @pl.when(hit == 0)
                def _():
                    pltpu.make_async_copy(zero, dst, sem).start()

    for start in (True, False):
        put(col_out, col_sem, x * ANCESTORS, ANCESTORS, False, start)
        put(row_out, row_sem, c * 2, 2, True, start)
    diag_copy.wait()


def body(stored_inverse, lhat, diag_inverse, ancestors):
    rows, cols = stored_inverse.shape
    stored = stored_inverse.reshape(rows // BLOCK, BLOCK, cols)
    anywhere = pl.BlockSpec(memory_space=pl.ANY)
    vmem = pl.BlockSpec(memory_space=pltpu.VMEM)
    smem = pl.BlockSpec(memory_space=pltpu.SMEM)
    dma = pltpu.SemaphoreType.DMA
    width = SUPERS * BLOCK
    pieces = (SIDE, SIDE, SIDE, QUARTER, BLOCK)
    square = (SUPERS, ANCESTORS, BLOCK, BLOCK)
    gather_sems = [dma, dma((3,)), dma((3, 3)), dma((3, 3))]
    tiles, diag = pl.pallas_call(
        kernel,
        out_shape=(
            pltpu.VMEM((SUPERS, ANCESTORS + 1, BLOCK, BLOCK), BF16),
            pltpu.VMEM(diag_inverse.shape, BF16),
        ),
        in_specs=[anywhere] * 4,
        out_specs=(vmem, vmem),
        scratch_shapes=[
            pltpu.SMEM(ancestors.shape, jnp.int32),
            pltpu.VMEM(diag_inverse.shape, BF16),
            pltpu.VMEM(pieces, BF16),
            pltpu.VMEM((rows // BLOCK, BLOCK, cols), BF16),
            pltpu.VMEM((SUPERS, ANCESTORS, SIDE, 2, QUARTER, BLOCK), BF16),
            pltpu.VMEM(square, BF16),
            pltpu.VMEM((SUPERS, SIDE, 2, QUARTER, BLOCK), BF16),
            pltpu.VMEM((SUPERS, SIDE - 1, 2, QUARTER, BLOCK), BF16),
            pltpu.VMEM((SUPERS, 2, QUARTER, BLOCK), BF16),
            pltpu.VMEM((SLOTS, QUARTER, BLOCK), BF16),
            pltpu.VMEM((PLANE, QUARTER, BLOCK), BF16),
            pltpu.VMEM(pieces, BF16),
            pltpu.VMEM(pieces, BF16),
            pltpu.VMEM(square, BF16),
            pltpu.VMEM((SUPERS, SIDE, QUARTER, BLOCK), BF16),
            pltpu.VMEM((SUPERS, BLOCK, BLOCK), BF16),
            pltpu.VMEM((SUPERS, 3, BLOCK, BLOCK), BF16),
            pltpu.VMEM((SUPERS, 3, BLOCK, BLOCK), BF16),
            pltpu.VMEM(ancestors.shape, jnp.int32),
            pltpu.SMEM(ancestors.shape, jnp.int32),
            pltpu.VMEM((PIECES * PIECE, 16, 128), BF16),
            dma((4,)), dma((2,)), *gather_sems, *gather_sems,
            dma, dma((SUPERS,)), dma, dma, dma, dma, dma((3,)), dma((3,)), dma((SUPERS,)), dma((SUPERS,)),
        ],
        compiler_params=pltpu.CompilerParams(
            collective_id=0, has_side_effects=True, vmem_limit_bytes=VMEM_LIMIT
        ),
        name="selected_inverse",
    )(ancestors, lhat, stored, diag_inverse)
    return pl.pallas_call(
        place,
        out_shape=(
            jax.ShapeDtypeStruct((1, rows, width), BF16),
            jax.ShapeDtypeStruct((1, cols, width), BF16),
            jax.ShapeDtypeStruct(diag_inverse.shape, BF16),
        ),
        in_specs=[smem, vmem, vmem],
        out_specs=(anywhere, anywhere, anywhere),
        scratch_shapes=[
            pltpu.VMEM((BLOCK, BLOCK), BF16),
            dma((SUPERS, ANCESTORS)), dma((SUPERS, 2)), dma,
        ],
        compiler_params=pltpu.CompilerParams(vmem_limit_bytes=VMEM_LIMIT // 8),
        name="placed_tiles",
    )(ancestors, tiles, diag)


def solution(mesh):
    return jax.shard_map(
        body,
        mesh=mesh,
        in_specs=(
            P("prow", "pcol"),
            P("layer", ("prow", "pcol"), None),
            P("layer", None, None, None),
            P("layer", None, None),
        ),
        out_specs=(
            P("layer", "prow", None),
            P("layer", "pcol", None),
            P("layer", None, None, None),
        ),
        check_vma=False,
    )
```

```python
import jax
import jax.numpy as jnp
from jax import lax
from jax.experimental import pallas as pl
from jax.experimental.pallas import tpu as pltpu
from jax.sharding import PartitionSpec as P

BLOCK = 256
ANCESTORS = 8
SUPERS = 2
TOP_BLOCKS = 28
SIDE = 4
PLANE = 16
PIECES = 64
QUARTER = 64
SLOTS = SUPERS * ANCESTORS
LAST = ANCESTORS - 1
MESH = pl.DeviceIdType.MESH
BF16 = jnp.bfloat16
F32 = jnp.float32
VMEM_LIMIT = 60 << 20

HOPS = (2, 1, 3)
ARRIVALS = (1, 3, 2)
NEXT = {"x": "y", "y": "z", "z": "x"}
WAY = {"x": 0, "y": 1, "z": 2}
PAIRS = sorted(((h, g) for h in ARRIVALS for g in ARRIVALS), key=lambda pair: pair.count(2))
UNIT = 16 * 128
PIECE = QUARTER * BLOCK // UNIT


class Gather:
    def __init__(self, buf, dims, me, layer, wait, send, first, second, third):
        self.buf, self.dims, self.me, self.layer, self.wait = buf, dims, me, layer, wait
        self.send, self.first, self.second, self.third = send, first, second, third

    def moved(self, **hops):
        at = dict(self.me)
        for axis, hop in hops.items():
            at[axis] = (self.me[axis] + SIDE + hop) % SIDE
        return at

    def index(self, at):
        return tuple(at[d] for d in self.dims)

    def pass_on(self, at, axis, hop, sem):
        piece = self.buf.at[self.index(at)]
        to = self.moved(**{axis: hop})
        pltpu.make_async_remote_copy(
            src_ref=piece, dst_ref=piece, send_sem=self.send, recv_sem=sem,
            device_id=(self.layer, to["x"], to["z"] * SIDE + to["y"]), device_id_type=MESH,
        ).start()

    def start(self):
        for hop in HOPS:
            for n, axis in enumerate("xyz"):
                self.pass_on(self.me, axis, hop, self.first.at[n, hop - 1])

    def after_first(self):
        for hop in ARRIVALS:
            for n, axis in enumerate("xyz"):
                self.wait(self.first.at[n, hop - 1], PIECE)
                source = self.moved(**{axis: -hop})
                for to in HOPS:
                    self.pass_on(source, NEXT[axis], to, self.second.at[n, hop - 1, to - 1])

    def after_second(self):
        for pair, (hop, then) in enumerate(PAIRS):
            for n, axis in enumerate("xyz"):
                self.wait(self.second.at[n, hop - 1, then - 1], PIECE)
                by = NEXT[axis]
                source = self.moved(**{axis: -hop, by: -then})
                last = next(f for f in ARRIVALS if (hop + then + f) % 3 == WAY[axis])
                self.pass_on(source, NEXT[by], last, self.third.at[pair])

    def nearer(self):
        i, j, k = self.dims
        yield (self.me[i],)
        for hop in ARRIVALS:
            yield self.moved(**{i: hop})[i], self.me[j]
        for hop in ARRIVALS:
            for then in ARRIVALS:
                at = self.moved(**{i: hop, j: then})
                yield self.index(at)

    def finish(self, act=None):
        for pair, (hop, then) in enumerate(PAIRS):
            self.wait(self.third.at[pair], 3 * PIECE)
            if act is not None:
                for axis in "xyz":
                    by = NEXT[axis]
                    last = next(f for f in ARRIVALS if (hop + then + f) % 3 == WAY[axis])
                    act(self.index(self.moved(**{axis: -hop, by: -then, NEXT[by]: -last})))

    def wait_sent(self):
        self.wait(self.send, (PIECES - 1) * PIECE)


def kernel(
    anc_any, panel_any, g_any, dinv_any,
    tiles, diag,
    anc, dinv, panels, g_own, g_pick, panel_t, partial, partial_in, summed, staged, moved, slots,
    other_slots, diag_now, diag_in, anc_in, anc_other, measure,
    in_sem, anc_sem,
    send1, first1, second1, third1, send2, first2, second2, third2,
    x_send, x_recv, c_send, c_recv, a_send, a_recv, d_send, d_recv,
):
    layer = lax.axis_index("layer")
    x = lax.axis_index("prow")
    c = lax.axis_index("pcol")
    z = c // SIDE
    y = c % SIDE
    me = {"x": x, "y": y, "z": z}
    sibling = (1 - layer, x, c)

    def wait(sem, count):
        ref = measure.at[pl.ds(0, count)]
        pltpu.make_async_copy(ref, ref, sem).wait()

    def to_sibling(src, dst, send, recv):
        return pltpu.make_async_remote_copy(
            src_ref=src, dst_ref=dst, send_sem=send, recv_sem=recv, device_id=sibling, device_id_type=MESH
        )

    panel_load = pltpu.make_async_copy(panel_any, panels.at[x, z, pl.ds(y, 1)], in_sem.at[0])
    anc_load = pltpu.make_async_copy(anc_any, anc, in_sem.at[1])
    dinv_load = pltpu.make_async_copy(dinv_any, dinv, in_sem.at[2])
    g_load = pltpu.make_async_copy(g_any, g_own, in_sem.at[3])
    panel_load.start()
    anc_load.start()
    g_load.start()
    dinv_load.start()

    barrier = pltpu.get_barrier_semaphore()

    def greet_plane(step, carry):
        pl.semaphore_signal(barrier, inc=1, device_id=(layer, x, (c + step) % PLANE), device_id_type=MESH)
        return carry

    def greet_line(step, carry):
        pl.semaphore_signal(barrier, inc=1, device_id=(layer, (x + step) % SIDE, c), device_id_type=MESH)
        return carry

    lax.fori_loop(1, PLANE, greet_plane, 0)
    lax.fori_loop(1, SIDE, greet_line, 0)
    pl.semaphore_signal(barrier, inc=1, device_id=sibling, device_id_type=MESH)
    pl.semaphore_wait(barrier, PLANE - 1 + SIDE - 1 + 1)

    gather1 = Gather(panels, ("x", "z", "y"), me, layer, wait, send1, first1, second1, third1)
    gather2 = Gather(slots, ("z", "y", "x"), me, layer, wait, send2, first2, second2, third2)
    panel_load.wait()
    gather1.start()
    anc_copy = to_sibling(anc_any, anc_in, anc_sem.at[0], anc_sem.at[1])
    anc_copy.start()
    anc_load.wait()
    dinv_load.wait()
    g_load.wait()

    def pick_blocks(k):
        def pick(p, carry):
            at = anc[0, k, p] - x * ANCESTORS
            here = jnp.logical_and(at >= 0, at < ANCESTORS)
            block = g_own[jnp.clip(at, 0, ANCESTORS - 1)]
            block = jnp.where(here, block, jnp.zeros_like(block))
            turned = block.T
            for b in range(2):
                for q in range(SIDE):
                    first = b * BLOCK + q * QUARTER
                    g_pick[k, p, q, b] = turned[first:first + QUARTER]
            return carry
        lax.fori_loop(0, ANCESTORS, pick, 0)

    def tile_of(ref, s):
        return ref[s // SIDE, s % SIDE].reshape(BLOCK, BLOCK)

    def multiply(k):
        total = jnp.zeros((2 * BLOCK, BLOCK), F32)
        for p in range(ANCESTORS):
            total += jnp.dot(
                g_pick[k, p].reshape(2 * BLOCK, BLOCK), tile_of(panels, k * ANCESTORS + p),
                preferred_element_type=F32,
            )
        partial[k] = total.astype(BF16).reshape(SIDE, 2, QUARTER, BLOCK)

    def start_reduce(k):
        for hop in HOPS:
            to = (x + hop) % SIDE
            pltpu.make_async_remote_copy(
                src_ref=partial.at[k, to], dst_ref=partial_in.at[k, hop - 1],
                send_sem=x_send, recv_sem=x_recv.at[k],
                device_id=(layer, to, c), device_id_type=MESH,
            ).start()

    def turn_panels():
        for k in range(SUPERS):
            def turn(p, carry):
                s = k * ANCESTORS + p
                panel_t[k, p] = tile_of(panels, s).T
                return carry
            lax.fori_loop(0, ANCESTORS, turn, 0)

    def start_move(k):
        wait(x_recv.at[k], 3 * 2 * PIECE)
        total = partial[k, x].astype(F32)
        for hop in HOPS:
            total += partial_in[k, hop - 1].astype(F32)
        summed[k] = total.astype(BF16)
        for q in range(ANCESTORS):
            staged[k * ANCESTORS + q] = summed[k, jnp.clip(anc[0, k, q] - 2 * c, 0, 1)]

        def send(step, carry):
            to = k * ANCESTORS + (c + step) % ANCESTORS

            @pl.when(to != c)
            def _():
                pltpu.make_async_remote_copy(
                    src_ref=staged.at[to], dst_ref=moved.at[c], send_sem=c_send, recv_sem=c_recv,
                    device_id=(layer, x, to), device_id_type=MESH,
                ).start()
            return carry
        lax.fori_loop(0, ANCESTORS, send, 0)

    def end_move():
        moved[c] = staged[c]
        wait(c_recv, (PLANE - 1) * PIECE)
        holder = anc[0, c // ANCESTORS, c % ANCESTORS] // 2
        slots[z, y, x] = moved[holder]

    gather1.after_first()
    pick_blocks(0)
    gather1.after_second()
    pick_blocks(1)
    gather1.finish()
    multiply(0)
    start_reduce(0)
    multiply(1)
    start_reduce(1)
    turn_panels()

    anc_copy.wait_recv()
    to_smem = pltpu.make_async_copy(anc_in, anc_other, in_sem.at[1])
    to_smem.start()
    to_smem.wait()
    start_move(0)
    start_move(1)
    end_move()
    gather2.start()

    parents, places = [], []
    for k in range(SUPERS):
        parent = jnp.clip(anc[0, k, LAST] - TOP_BLOCKS, 0, SUPERS - 1)
        found = []
        for q in range(LAST):
            at = jnp.int32(0)
            for j in range(ANCESTORS):
                at = jnp.where(anc_other[0, parent, j] == anc[0, k, q], j, at)
            found.append(parent * ANCESTORS + at)
        parents.append(parent)
        places.append(found)

    gather2.after_first()
    gather2.after_second()

    def pass_on(part):
        to_sibling(slots.at[part], other_slots.at[part], a_send, a_recv).start()

    d_copy = to_sibling(diag_now, diag_in, d_send, d_recv)

    def matrix(a, b):
        return jnp.dot(a, b, preferred_element_type=F32)

    @pl.when(layer == 0)
    def _():
        for part in gather2.nearer():
            pass_on(part)
        gather2.finish(pass_on)
        for k in range(SUPERS):
            total = dinv[0, k].astype(F32)
            for q in range(ANCESTORS):
                total += matrix(panel_t[k, q], tile_of(slots, k * ANCESTORS + q))
            diag_now[k] = total.astype(BF16)
        d_copy.start()
        for k in range(SUPERS):
            diag[0, k] = diag_now[k]
            for q in range(ANCESTORS):
                tiles[k, q] = -tile_of(slots, k * ANCESTORS + q)
        wait(a_send, PIECES * PIECE)
        d_copy.wait_send()

    @pl.when(layer == 1)
    def _():
        gather2.finish()
        sums, edges = [], []
        for k in range(SUPERS):
            total = dinv[0, k].astype(F32)
            for q in range(LAST):
                total += matrix(panel_t[k, q], tile_of(slots, k * ANCESTORS + q))
            sums.append(total)
            edges.append(tile_of(panels, k * ANCESTORS + LAST))
        wait(a_recv, PIECES * PIECE)
        crossed = []
        for k in range(SUPERS):
            total = jnp.zeros((BLOCK, BLOCK), F32)
            for q in range(LAST):
                tile = tile_of(other_slots, places[k][q])
                total += matrix(panel_t[k, q], tile)
                old = tile_of(slots, k * ANCESTORS + q).astype(F32)
                tiles[k, q] = (matrix(tile, edges[k]) - old).astype(BF16)
            crossed.append(total)
        d_copy.wait_recv()
        for k in range(SUPERS):
            above = diag_in[parents[k]]
            turned = crossed[k].T
            corner = (turned - matrix(above, edges[k])).astype(BF16)
            tiles[k, LAST] = corner
            tiles[k, ANCESTORS] = (turned - matrix(above.T, edges[k])).astype(BF16)
            total = sums[k] - matrix(crossed[k].astype(BF16), edges[k])
            diag[0, k] = (total - matrix(panel_t[k, LAST], corner)).astype(BF16)

    anc_copy.wait_send()
    gather1.wait_sent()
    gather2.wait_sent()
    wait(x_send, SUPERS * 3 * 2 * PIECE)
    wait(c_send, (PLANE - 1) * PIECE)


def place(anc, tiles, diag, col_out, row_out, diag_out, zero, col_sem, row_sem, diag_sem):
    layer = lax.axis_index("layer")
    x = lax.axis_index("prow")
    c = lax.axis_index("pcol")
    zero[...] = jnp.zeros_like(zero)
    diag_copy = pltpu.make_async_copy(diag, diag_out, diag_sem)
    diag_copy.start()

    def put(out, sems, first, blocks, row_side, start):
        for k in range(SUPERS):
            for j in range(blocks):
                dst = out.at[0, pl.ds(j * BLOCK, BLOCK), pl.ds(k * BLOCK, BLOCK)]
                sem = sems.at[k, j]
                if not start:
                    pltpu.make_async_copy(zero, dst, sem).wait()
                    continue
                at = jnp.int32(0)
                hit = jnp.int32(0)
                for q in range(ANCESTORS):
                    same = anc[0, k, q] == first + j
                    at = jnp.where(same, q, at)
                    hit = jnp.where(same, 1, hit)
                if row_side:
                    turned = jnp.logical_and(layer == 1, at == ANCESTORS - 1)
                    at = jnp.where(turned, ANCESTORS, at)

                @pl.when(hit > 0)
                def _():
                    pltpu.make_async_copy(tiles.at[k, at], dst, sem).start()

                @pl.when(hit == 0)
                def _():
                    pltpu.make_async_copy(zero, dst, sem).start()

    for start in (True, False):
        put(col_out, col_sem, x * ANCESTORS, ANCESTORS, False, start)
        put(row_out, row_sem, c * 2, 2, True, start)
    diag_copy.wait()


def body(stored_inverse, lhat, diag_inverse, ancestors):
    rows, cols = stored_inverse.shape
    stored = stored_inverse.reshape(rows // BLOCK, BLOCK, cols)
    anywhere = pl.BlockSpec(memory_space=pl.ANY)
    vmem = pl.BlockSpec(memory_space=pltpu.VMEM)
    smem = pl.BlockSpec(memory_space=pltpu.SMEM)
    dma = pltpu.SemaphoreType.DMA
    width = SUPERS * BLOCK
    pieces = (SIDE, SIDE, SIDE, QUARTER, BLOCK)
    gather_sems = [dma, dma((3, 3)), dma((3, 3, 3)), dma((len(PAIRS),))]
    tiles, diag = pl.pallas_call(
        kernel,
        out_shape=(
            pltpu.VMEM((SUPERS, ANCESTORS + 1, BLOCK, BLOCK), BF16),
            pltpu.VMEM(diag_inverse.shape, BF16),
        ),
        in_specs=[anywhere] * 4,
        out_specs=(vmem, vmem),
        scratch_shapes=[
            pltpu.SMEM(ancestors.shape, jnp.int32),
            pltpu.VMEM(diag_inverse.shape, BF16),
            pltpu.VMEM(pieces, BF16),
            pltpu.VMEM((rows // BLOCK, BLOCK, cols), BF16),
            pltpu.VMEM((SUPERS, ANCESTORS, SIDE, 2, QUARTER, BLOCK), BF16),
            pltpu.VMEM((SUPERS, ANCESTORS, BLOCK, BLOCK), BF16),
            pltpu.VMEM((SUPERS, SIDE, 2, QUARTER, BLOCK), BF16),
            pltpu.VMEM((SUPERS, SIDE - 1, 2, QUARTER, BLOCK), BF16),
            pltpu.VMEM((SUPERS, 2, QUARTER, BLOCK), BF16),
            pltpu.VMEM((SLOTS, QUARTER, BLOCK), BF16),
            pltpu.VMEM((PLANE, QUARTER, BLOCK), BF16),
            pltpu.VMEM(pieces, BF16),
            pltpu.VMEM(pieces, BF16),
            pltpu.VMEM((SUPERS, BLOCK, BLOCK), BF16),
            pltpu.VMEM((SUPERS, BLOCK, BLOCK), BF16),
            pltpu.VMEM(ancestors.shape, jnp.int32),
            pltpu.SMEM(ancestors.shape, jnp.int32),
            pltpu.VMEM((PIECES * PIECE, 16, 128), BF16),
            dma((4,)), dma((2,)), *gather_sems, *gather_sems,
            dma, dma((SUPERS,)), dma, dma, dma, dma, dma, dma,
        ],
        compiler_params=pltpu.CompilerParams(
            collective_id=0, has_side_effects=True, vmem_limit_bytes=VMEM_LIMIT
        ),
        name="selected_inverse",
    )(ancestors, lhat, stored, diag_inverse)
    return pl.pallas_call(
        place,
        out_shape=(
            jax.ShapeDtypeStruct((1, rows, width), BF16),
            jax.ShapeDtypeStruct((1, cols, width), BF16),
            jax.ShapeDtypeStruct(diag_inverse.shape, BF16),
        ),
        in_specs=[smem, vmem, vmem],
        out_specs=(anywhere, anywhere, anywhere),
        scratch_shapes=[
            pltpu.VMEM((BLOCK, BLOCK), BF16),
            dma((SUPERS, ANCESTORS)), dma((SUPERS, 2)), dma,
        ],
        compiler_params=pltpu.CompilerParams(vmem_limit_bytes=VMEM_LIMIT // 8),
        name="placed_tiles",
    )(ancestors, tiles, diag)


def solution(mesh):
    return jax.shard_map(
        body,
        mesh=mesh,
        in_specs=(
            P("prow", "pcol"),
            P("layer", ("prow", "pcol"), None),
            P("layer", None, None, None),
            P("layer", None, None),
        ),
        out_specs=(
            P("layer", "prow", None),
            P("layer", "pcol", None),
            P("layer", None, None, None),
        ),
        check_vma=False,
    )
```

```python
import jax
import jax.numpy as jnp
from jax import lax
from jax.experimental import pallas as pl
from jax.experimental.pallas import tpu as pltpu
from jax.sharding import PartitionSpec as P

BLOCK = 256
ANCESTORS = 8
SUPERS = 2
TOP_BLOCKS = 28
SIDE = 4
PLANE = 16
PIECES = 64
QUARTER = 64
SLOTS = SUPERS * ANCESTORS
LAST = ANCESTORS - 1
MESH = pl.DeviceIdType.MESH
BF16 = jnp.bfloat16
F32 = jnp.float32
VMEM_LIMIT = 60 << 20

HOPS = (2, 1, 3)
ARRIVALS = (1, 3, 2)
NEXT = {"x": "y", "y": "z", "z": "x"}
WAY = {"x": 0, "y": 1, "z": 2}
PAIRS = sorted(((h, g) for h in ARRIVALS for g in ARRIVALS), key=lambda pair: pair.count(2))
UNIT = 16 * 128
PIECE = QUARTER * BLOCK // UNIT


class Gather:
    def __init__(self, buf, dims, me, layer, wait, send, first, second, third):
        self.buf, self.dims, self.me, self.layer, self.wait = buf, dims, me, layer, wait
        self.send, self.first, self.second, self.third = send, first, second, third

    def moved(self, **hops):
        at = dict(self.me)
        for axis, hop in hops.items():
            at[axis] = (self.me[axis] + SIDE + hop) % SIDE
        return at

    def index(self, at):
        return tuple(at[d] for d in self.dims)

    def pass_on(self, at, axis, hop, sem):
        piece = self.buf.at[self.index(at)]
        to = self.moved(**{axis: hop})
        pltpu.make_async_remote_copy(
            src_ref=piece, dst_ref=piece, send_sem=self.send, recv_sem=sem,
            device_id=(self.layer, to["x"], to["z"] * SIDE + to["y"]), device_id_type=MESH,
        ).start()

    def start(self):
        for hop in HOPS:
            for n, axis in enumerate("xyz"):
                self.pass_on(self.me, axis, hop, self.first.at[n, hop - 1])

    def after_first(self):
        for hop in ARRIVALS:
            for n, axis in enumerate("xyz"):
                self.wait(self.first.at[n, hop - 1], PIECE)
                source = self.moved(**{axis: -hop})
                for to in HOPS:
                    self.pass_on(source, NEXT[axis], to, self.second.at[n, hop - 1, to - 1])

    def after_second(self):
        for pair, (hop, then) in enumerate(PAIRS):
            for n, axis in enumerate("xyz"):
                self.wait(self.second.at[n, hop - 1, then - 1], PIECE)
                by = NEXT[axis]
                source = self.moved(**{axis: -hop, by: -then})
                last = next(f for f in ARRIVALS if (hop + then + f) % 3 == WAY[axis])
                self.pass_on(source, NEXT[by], last, self.third.at[pair])

    def nearer(self):
        i, j, k = self.dims
        yield (self.me[i],)
        for hop in ARRIVALS:
            yield self.moved(**{i: hop})[i], self.me[j]
        for hop in ARRIVALS:
            for then in ARRIVALS:
                at = self.moved(**{i: hop, j: then})
                yield self.index(at)

    def finish(self, act=None):
        for pair, (hop, then) in enumerate(PAIRS):
            self.wait(self.third.at[pair], 3 * PIECE)
            if act is not None:
                for axis in "xyz":
                    by = NEXT[axis]
                    last = next(f for f in ARRIVALS if (hop + then + f) % 3 == WAY[axis])
                    act(self.index(self.moved(**{axis: -hop, by: -then, NEXT[by]: -last})))

    def wait_sent(self):
        self.wait(self.send, (PIECES - 1) * PIECE)


def kernel(
    anc_any, panel_any, g_any, dinv_any,
    tiles, diag, anc,
    dinv, panels, g_own, g_pick, panel_t, partial, partial_in, summed, staged, moved, slots,
    other_slots, diag_now, diag_in, anc_in, anc_other, measure,
    in_sem, anc_sem,
    send1, first1, second1, third1, send2, third2,
    x_send, x_recv, c_send, c_recv, a_send, a_recv, d_send, d_recv,
):
    layer = lax.axis_index("layer")
    x = lax.axis_index("prow")
    c = lax.axis_index("pcol")
    z = c // SIDE
    y = c % SIDE
    me = {"x": x, "y": y, "z": z}
    sibling = (1 - layer, x, c)

    def wait(sem, count):
        ref = measure.at[pl.ds(0, count)]
        pltpu.make_async_copy(ref, ref, sem).wait()

    def to_sibling(src, dst, send, recv):
        return pltpu.make_async_remote_copy(
            src_ref=src, dst_ref=dst, send_sem=send, recv_sem=recv, device_id=sibling, device_id_type=MESH
        )

    barrier = pltpu.get_barrier_semaphore()
    greeted = [(layer, (x + step) % SIDE, c) for step in range(1, SIDE)]
    greeted += [(layer, x, (c + step) % PLANE) for step in range(1, PLANE)]
    greeted.append(sibling)
    for device in greeted:
        pl.semaphore_signal(barrier, inc=1, device_id=device, device_id_type=MESH)
    panel_load = pltpu.make_async_copy(panel_any, panels.at[x, z, pl.ds(y, 1)], in_sem.at[0])
    anc_load = pltpu.make_async_copy(anc_any, anc, in_sem.at[1])
    dinv_load = pltpu.make_async_copy(dinv_any, dinv, in_sem.at[2])
    g_load = pltpu.make_async_copy(g_any, g_own, in_sem.at[3])
    panel_load.start()
    anc_load.start()
    g_load.start()
    dinv_load.start()

    pl.semaphore_wait(barrier, len(greeted))

    gather1 = Gather(panels, ("x", "z", "y"), me, layer, wait, send1, first1, second1, third1)
    gather2 = Gather(slots, ("z", "y", "x"), me, layer, wait, send2, first1, second1, third2)
    panel_load.wait()
    gather1.start()
    anc_copy = to_sibling(anc_any, anc_in, anc_sem.at[0], anc_sem.at[1])
    anc_copy.start()
    anc_load.wait()
    dinv_load.wait()
    g_load.wait()

    def pick_blocks(k):
        def pick(p, carry):
            at = anc[0, k, p] - x * ANCESTORS
            here = jnp.logical_and(at >= 0, at < ANCESTORS)
            block = g_own[jnp.clip(at, 0, ANCESTORS - 1)]
            block = jnp.where(here, block, jnp.zeros_like(block))
            turned = block.T
            for b in range(2):
                for q in range(SIDE):
                    first = b * BLOCK + q * QUARTER
                    g_pick[k, p, q, b] = turned[first:first + QUARTER]
            return carry
        lax.fori_loop(0, ANCESTORS, pick, 0)

    def tile_of(ref, s):
        return ref[s // SIDE, s % SIDE].reshape(BLOCK, BLOCK)

    def multiply(k):
        total = jnp.zeros((2 * BLOCK, BLOCK), F32)
        for p in range(ANCESTORS):
            total += jnp.dot(
                g_pick[k, p].reshape(2 * BLOCK, BLOCK), tile_of(panels, k * ANCESTORS + p),
                preferred_element_type=F32,
            )
        partial[k] = total.astype(BF16).reshape(SIDE, 2, QUARTER, BLOCK)

    def start_reduce(k):
        for hop in HOPS:
            to = (x + hop) % SIDE
            pltpu.make_async_remote_copy(
                src_ref=partial.at[k, to], dst_ref=partial_in.at[k, hop - 1],
                send_sem=x_send, recv_sem=x_recv.at[k],
                device_id=(layer, to, c), device_id_type=MESH,
            ).start()

    def turn_panels():
        for k in range(SUPERS):
            def turn(p, carry):
                s = k * ANCESTORS + p
                panel_t[k, p] = tile_of(panels, s).T
                return carry
            lax.fori_loop(0, ANCESTORS, turn, 0)

    def start_move(k):
        wait(x_recv.at[k], 3 * 2 * PIECE)
        total = partial[k, x].astype(F32)
        for hop in HOPS:
            total += partial_in[k, hop - 1].astype(F32)
        summed[k] = total.astype(BF16)
        for q in range(ANCESTORS):
            staged[k * ANCESTORS + q] = summed[k, jnp.clip(anc[0, k, q] - 2 * c, 0, 1)]

        def send(step, carry):
            to = k * ANCESTORS + (c + step) % ANCESTORS

            @pl.when(to != c)
            def _():
                pltpu.make_async_remote_copy(
                    src_ref=staged.at[to], dst_ref=moved.at[c], send_sem=c_send, recv_sem=c_recv,
                    device_id=(layer, x, to), device_id_type=MESH,
                ).start()
            return carry
        lax.fori_loop(0, ANCESTORS, send, 0)

    def end_move():
        moved[c] = staged[c]
        wait(c_recv, (PLANE - 1) * PIECE)
        holder = anc[0, c // ANCESTORS, c % ANCESTORS] // 2
        slots[z, y, x] = moved[holder]

    gather1.after_first()
    pick_blocks(0)
    gather1.after_second()
    pick_blocks(1)
    gather1.finish()
    multiply(0)
    start_reduce(0)
    multiply(1)
    start_reduce(1)
    turn_panels()

    anc_copy.wait_recv()
    to_smem = pltpu.make_async_copy(anc_in, anc_other, in_sem.at[1])
    to_smem.start()
    to_smem.wait()
    start_move(0)
    start_move(1)
    end_move()
    gather2.start()

    parents, places = [], []
    for k in range(SUPERS):
        parent = jnp.clip(anc[0, k, LAST] - TOP_BLOCKS, 0, SUPERS - 1)
        found = []
        for q in range(LAST):
            at = jnp.int32(0)
            for j in range(ANCESTORS):
                at = jnp.where(anc_other[0, parent, j] == anc[0, k, q], j, at)
            found.append(parent * ANCESTORS + at)
        parents.append(parent)
        places.append(found)

    gather2.after_first()
    gather2.after_second()

    def pass_on(part):
        to_sibling(slots.at[part], other_slots.at[part], a_send, a_recv).start()

    d_copy = to_sibling(diag_now, diag_in, d_send, d_recv)

    def matrix(a, b):
        return jnp.dot(a, b, preferred_element_type=F32)

    @pl.when(layer == 0)
    def _():
        for part in gather2.nearer():
            pass_on(part)
        gather2.finish(pass_on)
        for k in range(SUPERS):
            total = dinv[0, k].astype(F32)
            for q in range(ANCESTORS):
                total += matrix(panel_t[k, q], tile_of(slots, k * ANCESTORS + q))
            diag_now[k] = total.astype(BF16)
        d_copy.start()
        for k in range(SUPERS):
            diag[0, k] = diag_now[k]
            for q in range(ANCESTORS):
                tiles[k, q] = -tile_of(slots, k * ANCESTORS + q)
        wait(a_send, PIECES * PIECE)
        d_copy.wait_send()

    @pl.when(layer == 1)
    def _():
        gather2.finish()
        sums, edges = [], []
        for k in range(SUPERS):
            total = dinv[0, k].astype(F32)
            for q in range(LAST):
                total += matrix(panel_t[k, q], tile_of(slots, k * ANCESTORS + q))
            sums.append(total)
            edges.append(tile_of(panels, k * ANCESTORS + LAST))
        wait(a_recv, PIECES * PIECE)
        crossed = []
        for k in range(SUPERS):
            total = jnp.zeros((BLOCK, BLOCK), F32)
            for q in range(LAST):
                tile = tile_of(other_slots, places[k][q])
                total += matrix(panel_t[k, q], tile)
                old = tile_of(slots, k * ANCESTORS + q).astype(F32)
                tiles[k, q] = (matrix(tile, edges[k]) - old).astype(BF16)
            crossed.append(total)
        d_copy.wait_recv()
        for k in range(SUPERS):
            above = diag_in[parents[k]]
            turned = crossed[k].T
            corner = (turned - matrix(above, edges[k])).astype(BF16)
            tiles[k, LAST] = corner
            tiles[k, ANCESTORS] = (turned - matrix(above.T, edges[k])).astype(BF16)
            total = sums[k] - matrix(crossed[k].astype(BF16), edges[k])
            diag[0, k] = (total - matrix(panel_t[k, LAST], corner)).astype(BF16)

    anc_copy.wait_send()
    gather1.wait_sent()
    gather2.wait_sent()
    wait(x_send, SUPERS * 3 * 2 * PIECE)
    wait(c_send, (PLANE - 1) * PIECE)


def place(anc, tiles, diag, col_out, row_out, diag_out, zero, col_sem, row_sem, diag_sem):
    layer = lax.axis_index("layer")
    x = lax.axis_index("prow")
    c = lax.axis_index("pcol")
    zero[...] = jnp.zeros_like(zero)
    diag_copy = pltpu.make_async_copy(diag, diag_out, diag_sem)
    diag_copy.start()

    def put(out, sems, first, blocks, row_side, start):
        for k in range(SUPERS):
            for j in range(blocks):
                dst = out.at[0, pl.ds(j * BLOCK, BLOCK), pl.ds(k * BLOCK, BLOCK)]
                sem = sems.at[k, j]
                if not start:
                    pltpu.make_async_copy(zero, dst, sem).wait()
                    continue
                at = jnp.int32(0)
                hit = jnp.int32(0)
                for q in range(ANCESTORS):
                    same = anc[0, k, q] == first + j
                    at = jnp.where(same, q, at)
                    hit = jnp.where(same, 1, hit)
                if row_side:
                    turned = jnp.logical_and(layer == 1, at == ANCESTORS - 1)
                    at = jnp.where(turned, ANCESTORS, at)

                @pl.when(hit > 0)
                def _():
                    pltpu.make_async_copy(tiles.at[k, at], dst, sem).start()

                @pl.when(hit == 0)
                def _():
                    pltpu.make_async_copy(zero, dst, sem).start()

    for start in (True, False):
        put(col_out, col_sem, x * ANCESTORS, ANCESTORS, False, start)
        put(row_out, row_sem, c * 2, 2, True, start)
    diag_copy.wait()


def body(stored_inverse, lhat, diag_inverse, ancestors):
    rows, cols = stored_inverse.shape
    stored = stored_inverse.reshape(rows // BLOCK, BLOCK, cols)
    anywhere = pl.BlockSpec(memory_space=pl.ANY)
    vmem = pl.BlockSpec(memory_space=pltpu.VMEM)
    smem = pl.BlockSpec(memory_space=pltpu.SMEM)
    dma = pltpu.SemaphoreType.DMA
    width = SUPERS * BLOCK
    pieces = (SIDE, SIDE, SIDE, QUARTER, BLOCK)
    gather_sems = [dma, dma((3, 3)), dma((3, 3, 3)), dma((len(PAIRS),))]
    tiles, diag, lists = pl.pallas_call(
        kernel,
        out_shape=(
            pltpu.VMEM((SUPERS, ANCESTORS + 1, BLOCK, BLOCK), BF16),
            pltpu.VMEM(diag_inverse.shape, BF16),
            pltpu.SMEM(ancestors.shape, jnp.int32),
        ),
        in_specs=[anywhere] * 4,
        out_specs=(vmem, vmem, smem),
        scratch_shapes=[
            pltpu.VMEM(diag_inverse.shape, BF16),
            pltpu.VMEM(pieces, BF16),
            pltpu.VMEM((rows // BLOCK, BLOCK, cols), BF16),
            pltpu.VMEM((SUPERS, ANCESTORS, SIDE, 2, QUARTER, BLOCK), BF16),
            pltpu.VMEM((SUPERS, ANCESTORS, BLOCK, BLOCK), BF16),
            pltpu.VMEM((SUPERS, SIDE, 2, QUARTER, BLOCK), BF16),
            pltpu.VMEM((SUPERS, SIDE - 1, 2, QUARTER, BLOCK), BF16),
            pltpu.VMEM((SUPERS, 2, QUARTER, BLOCK), BF16),
            pltpu.VMEM((SLOTS, QUARTER, BLOCK), BF16),
            pltpu.VMEM((PLANE, QUARTER, BLOCK), BF16),
            pltpu.VMEM(pieces, BF16),
            pltpu.VMEM(pieces, BF16),
            pltpu.VMEM((SUPERS, BLOCK, BLOCK), BF16),
            pltpu.VMEM((SUPERS, BLOCK, BLOCK), BF16),
            pltpu.VMEM(ancestors.shape, jnp.int32),
            pltpu.SMEM(ancestors.shape, jnp.int32),
            pltpu.VMEM((PIECES * PIECE, 16, 128), BF16),
            dma((4,)), dma((2,)), *gather_sems, dma, dma((len(PAIRS),)),
            dma, dma((SUPERS,)), dma, dma, dma, dma, dma, dma,
        ],
        compiler_params=pltpu.CompilerParams(
            collective_id=0, has_side_effects=True, vmem_limit_bytes=VMEM_LIMIT
        ),
        name="selected_inverse",
    )(ancestors, lhat, stored, diag_inverse)
    return pl.pallas_call(
        place,
        out_shape=(
            jax.ShapeDtypeStruct((1, rows, width), BF16),
            jax.ShapeDtypeStruct((1, cols, width), BF16),
            jax.ShapeDtypeStruct(diag_inverse.shape, BF16),
        ),
        in_specs=[smem, vmem, vmem],
        out_specs=(anywhere, anywhere, anywhere),
        scratch_shapes=[
            pltpu.VMEM((BLOCK, BLOCK), BF16),
            dma((SUPERS, ANCESTORS)), dma((SUPERS, 2)), dma,
        ],
        compiler_params=pltpu.CompilerParams(vmem_limit_bytes=VMEM_LIMIT // 8),
        name="placed_tiles",
    )(lists, tiles, diag)


def solution(mesh):
    return jax.shard_map(
        body,
        mesh=mesh,
        in_specs=(
            P("prow", "pcol"),
            P("layer", ("prow", "pcol"), None),
            P("layer", None, None, None),
            P("layer", None, None),
        ),
        out_specs=(
            P("layer", "prow", None),
            P("layer", "pcol", None),
            P("layer", None, None, None),
        ),
        check_vma=False,
    )
```

```python
import jax
import jax.numpy as jnp
from jax import lax
from jax.experimental import pallas as pl
from jax.experimental.pallas import tpu as pltpu
from jax.sharding import PartitionSpec as P

BLOCK = 256
ANCESTORS = 8
SUPERS = 2
TOP_BLOCKS = 28
SIDE = 4
PLANE = 16
PIECES = 64
QUARTER = 64
SLOTS = SUPERS * ANCESTORS
LAST = ANCESTORS - 1
MESH = pl.DeviceIdType.MESH
BF16 = jnp.bfloat16
F32 = jnp.float32
VMEM_LIMIT = 60 << 20

HOPS = (2, 1, 3)
ARRIVALS = (1, 3, 2)
NEXT = {"x": "y", "y": "z", "z": "x"}
WAY = {"x": 0, "y": 1, "z": 2}
PAIRS = sorted(((h, g) for h in ARRIVALS for g in ARRIVALS), key=lambda pair: pair.count(2))
UNIT = 16 * 128
PIECE = QUARTER * BLOCK // UNIT


class Gather:
    def __init__(self, buf, dims, me, layer, wait, send, first, second, third):
        self.buf, self.dims, self.me, self.layer, self.wait = buf, dims, me, layer, wait
        self.send, self.first, self.second, self.third = send, first, second, third

    def moved(self, **hops):
        at = dict(self.me)
        for axis, hop in hops.items():
            at[axis] = (self.me[axis] + SIDE + hop) % SIDE
        return at

    def index(self, at):
        return tuple(at[d] for d in self.dims)

    def pass_on(self, at, axis, hop, sem):
        piece = self.buf.at[self.index(at)]
        to = self.moved(**{axis: hop})
        pltpu.make_async_remote_copy(
            src_ref=piece, dst_ref=piece, send_sem=self.send, recv_sem=sem,
            device_id=(self.layer, to["x"], to["z"] * SIDE + to["y"]), device_id_type=MESH,
        ).start()

    def start(self):
        for hop in HOPS:
            for n, axis in enumerate("xyz"):
                self.pass_on(self.me, axis, hop, self.first.at[n, hop - 1])

    def after_first(self):
        for hop in ARRIVALS:
            for n, axis in enumerate("xyz"):
                self.wait(self.first.at[n, hop - 1], PIECE)
                source = self.moved(**{axis: -hop})
                for to in HOPS:
                    self.pass_on(source, NEXT[axis], to, self.second.at[n, hop - 1, to - 1])

    def after_second(self):
        for hop, then in PAIRS:
            for n, axis in enumerate("xyz"):
                self.wait(self.second.at[n, hop - 1, then - 1], PIECE)
                by = NEXT[axis]
                source = self.moved(**{axis: -hop, by: -then})
                last = next(f for f in ARRIVALS if (hop + then + f) % 3 == WAY[axis])
                self.pass_on(source, NEXT[by], last, self.third)

    def finish(self):
        self.wait(self.third, 27 * PIECE)

    def wait_sent(self):
        self.wait(self.send, (PIECES - 1) * PIECE)


def kernel(
    anc_any, panel_any, g_any, dinv_any,
    tiles, diag, anc,
    dinv, panels, g_own, g_pick, panel_t, partial, partial_in, summed, staged, moved, slots,
    other_panel_t, other_dinv, other_piece, anc_in, anc_other, measure,
    in_sem, anc_sem,
    send1, first1, second1, third1, send2, third2,
    x_send, x_recv, c_send, c_recv, a_send, a_recv, m_send, m_recv, d_send, d_recv,
):
    layer = lax.axis_index("layer")
    x = lax.axis_index("prow")
    c = lax.axis_index("pcol")
    z = c // SIDE
    y = c % SIDE
    me = {"x": x, "y": y, "z": z}
    sibling = (1 - layer, x, c)

    def wait(sem, count):
        ref = measure.at[pl.ds(0, count)]
        pltpu.make_async_copy(ref, ref, sem).wait()

    def to_sibling(src, dst, send, recv):
        return pltpu.make_async_remote_copy(
            src_ref=src, dst_ref=dst, send_sem=send, recv_sem=recv, device_id=sibling, device_id_type=MESH
        )

    barrier = pltpu.get_barrier_semaphore()
    greeted = [(layer, (x + step) % SIDE, c) for step in range(1, SIDE)]
    greeted += [(layer, x, (c + step) % PLANE) for step in range(1, PLANE)]
    greeted.append(sibling)
    for device in greeted:
        pl.semaphore_signal(barrier, inc=1, device_id=device, device_id_type=MESH)
    panel_load = pltpu.make_async_copy(panel_any, panels.at[x, z, pl.ds(y, 1)], in_sem.at[0])
    anc_load = pltpu.make_async_copy(anc_any, anc, in_sem.at[1])
    dinv_load = pltpu.make_async_copy(dinv_any, dinv, in_sem.at[2])
    g_load = pltpu.make_async_copy(g_any, g_own, in_sem.at[3])
    panel_load.start()
    anc_load.start()
    g_load.start()
    dinv_load.start()

    pl.semaphore_wait(barrier, len(greeted))

    gather1 = Gather(panels, ("x", "z", "y"), me, layer, wait, send1, first1, second1, third1)
    gather2 = Gather(slots, ("z", "y", "x"), me, layer, wait, send2, first1, second1, third2)
    panel_load.wait()
    gather1.start()
    anc_copy = to_sibling(anc_any, anc_in, anc_sem.at[0], anc_sem.at[1])
    anc_copy.start()
    anc_load.wait()
    dinv_load.wait()
    g_load.wait()

    def parent_of(k):
        return jnp.clip(anc[0, k, LAST] - TOP_BLOCKS, 0, SUPERS - 1)

    def own_super(k):
        child = jnp.where(parent_of(0) == k, 0, 1)
        return jnp.where(layer == 0, k, child)

    def slot_block(k, q):
        return jnp.where(layer == 0, anc[0, k, q], anc_other[0, k, q])

    def pick_blocks(k):
        own = own_super(k)

        def pick(p, carry):
            at = anc[0, own, p] - x * ANCESTORS
            here = jnp.logical_and(at >= 0, at < ANCESTORS)
            block = g_own[jnp.clip(at, 0, ANCESTORS - 1)]
            block = jnp.where(here, block, jnp.zeros_like(block))
            turned = block.T
            for b in range(2):
                for q in range(SIDE):
                    first = b * BLOCK + q * QUARTER
                    g_pick[k, p, q, b] = turned[first:first + QUARTER]
            return carry
        lax.fori_loop(0, ANCESTORS, pick, 0)

    def tile_of(ref, s):
        return ref[s // SIDE, s % SIDE].reshape(BLOCK, BLOCK)

    def multiply(k):
        own = own_super(k)
        total = jnp.zeros((2 * BLOCK, BLOCK), F32)
        for p in range(ANCESTORS):
            total += jnp.dot(
                g_pick[k, p].reshape(2 * BLOCK, BLOCK), tile_of(panels, own * ANCESTORS + p),
                preferred_element_type=F32,
            )
        partial[k] = total.astype(BF16).reshape(SIDE, 2, QUARTER, BLOCK)

    def start_reduce(k):
        for hop in HOPS:
            to = (x + hop) % SIDE
            pltpu.make_async_remote_copy(
                src_ref=partial.at[k, to], dst_ref=partial_in.at[k, hop - 1],
                send_sem=x_send, recv_sem=x_recv.at[k],
                device_id=(layer, to, c), device_id_type=MESH,
            ).start()

    def turn_panels():
        for k in range(SUPERS):
            def turn(p, carry):
                s = k * ANCESTORS + p
                panel_t[k, p] = tile_of(panels, s).T
                return carry
            lax.fori_loop(0, ANCESTORS, turn, 0)

    def start_move(k):
        wait(x_recv.at[k], 3 * 2 * PIECE)
        total = partial[k, x].astype(F32)
        for hop in HOPS:
            total += partial_in[k, hop - 1].astype(F32)
        summed[k] = total.astype(BF16)
        for q in range(ANCESTORS):
            staged[k * ANCESTORS + q] = summed[k, jnp.clip(slot_block(k, q) - 2 * c, 0, 1)]

        def send(step, carry):
            to = k * ANCESTORS + (c + step) % ANCESTORS

            @pl.when(to != c)
            def _():
                pltpu.make_async_remote_copy(
                    src_ref=staged.at[to], dst_ref=moved.at[c], send_sem=c_send, recv_sem=c_recv,
                    device_id=(layer, x, to), device_id_type=MESH,
                ).start()
            return carry
        lax.fori_loop(0, ANCESTORS, send, 0)

    def end_move():
        moved[c] = staged[c]
        wait(c_recv, (PLANE - 1) * PIECE)
        piece = moved[slot_block(c // ANCESTORS, c % ANCESTORS) // 2]
        passed = to_sibling(slots.at[z, y, x], other_piece, a_send, a_recv)

        @pl.when(layer == 0)
        def _():
            slots[z, y, x] = piece
            passed.start()

        @pl.when(layer == 1)
        def _():
            passed.wait_recv()
            edge = tile_of(panels, own_super(c // ANCESTORS) * ANCESTORS + LAST)
            new = jnp.dot(other_piece[...], edge, preferred_element_type=F32)
            slots[z, y, x] = (new - piece.astype(F32)).astype(BF16)
        return passed

    m_copy = to_sibling(panel_t, other_panel_t, m_send, m_recv)
    d_copy = to_sibling(dinv, other_dinv, d_send, d_recv)

    gather1.after_first()
    pick_blocks(0)
    gather1.after_second()
    pick_blocks(1)
    gather1.finish()
    multiply(0)
    start_reduce(0)
    multiply(1)
    start_reduce(1)
    turn_panels()

    @pl.when(layer == 0)
    def _():
        m_copy.start()
        d_copy.start()

    anc_copy.wait_recv()
    to_smem = pltpu.make_async_copy(anc_in, anc_other, in_sem.at[1])
    to_smem.start()
    to_smem.wait()
    start_move(0)
    start_move(1)
    passed = end_move()
    gather2.start()

    parents, places = [], []
    for k in range(SUPERS):
        parent = parent_of(k)
        found = []
        for q in range(LAST):
            at = jnp.int32(0)
            for j in range(ANCESTORS):
                at = jnp.where(anc_other[0, parent, j] == anc[0, k, q], j, at)
            found.append(parent * ANCESTORS + at)
        parents.append(parent)
        places.append(found)

    gather2.after_first()
    gather2.after_second()

    def matrix(a, b):
        return jnp.dot(a, b, preferred_element_type=F32)

    @pl.when(layer == 0)
    def _():
        gather2.finish()
        for k in range(SUPERS):
            total = dinv[0, k].astype(F32)
            for q in range(ANCESTORS):
                tile = tile_of(slots, k * ANCESTORS + q)
                total += matrix(panel_t[k, q], tile)
                tiles[k, q] = -tile
            diag[0, k] = total.astype(BF16)
        passed.wait_send()
        m_copy.wait_send()
        d_copy.wait_send()

    @pl.when(layer == 1)
    def _():
        m_copy.wait_recv()
        d_copy.wait_recv()
        crossed, turned = [], []
        for k in range(SUPERS):
            edge = tile_of(panels, k * ANCESTORS + LAST)
            above = other_dinv[0, parents[k]]
            crossed.append(matrix(above, edge))
            turned.append(matrix(above.T, edge))
        gather2.finish()
        for k in range(SUPERS):
            total = jnp.zeros((BLOCK, BLOCK), F32)
            for p in range(ANCESTORS):
                total += matrix(other_panel_t[parents[k], p], tile_of(slots, parents[k] * ANCESTORS + p))
            corner = (-total - crossed[k]).astype(BF16)
            tiles[k, LAST] = corner
            tiles[k, ANCESTORS] = (-total - turned[k]).astype(BF16)
            total = dinv[0, k].astype(F32)
            for q in range(LAST):
                tile = tile_of(slots, places[k][q])
                total -= matrix(panel_t[k, q], tile)
                tiles[k, q] = tile
            diag[0, k] = (total - matrix(panel_t[k, LAST], corner)).astype(BF16)

    anc_copy.wait_send()
    gather1.wait_sent()
    gather2.wait_sent()
    wait(x_send, SUPERS * 3 * 2 * PIECE)
    wait(c_send, (PLANE - 1) * PIECE)


def place(anc, tiles, diag, col_out, row_out, diag_out, zero, col_sem, row_sem, diag_sem):
    layer = lax.axis_index("layer")
    x = lax.axis_index("prow")
    c = lax.axis_index("pcol")
    zero[...] = jnp.zeros_like(zero)
    diag_copy = pltpu.make_async_copy(diag, diag_out, diag_sem)
    diag_copy.start()

    def put(out, sems, first, blocks, row_side, start):
        for k in range(SUPERS):
            for j in range(blocks):
                dst = out.at[0, pl.ds(j * BLOCK, BLOCK), pl.ds(k * BLOCK, BLOCK)]
                sem = sems.at[k, j]
                if not start:
                    pltpu.make_async_copy(zero, dst, sem).wait()
                    continue
                at = jnp.int32(0)
                hit = jnp.int32(0)
                for q in range(ANCESTORS):
                    same = anc[0, k, q] == first + j
                    at = jnp.where(same, q, at)
                    hit = jnp.where(same, 1, hit)
                if row_side:
                    turned = jnp.logical_and(layer == 1, at == ANCESTORS - 1)
                    at = jnp.where(turned, ANCESTORS, at)

                @pl.when(hit > 0)
                def _():
                    pltpu.make_async_copy(tiles.at[k, at], dst, sem).start()

                @pl.when(hit == 0)
                def _():
                    pltpu.make_async_copy(zero, dst, sem).start()

    for start in (True, False):
        put(col_out, col_sem, x * ANCESTORS, ANCESTORS, False, start)
        put(row_out, row_sem, c * 2, 2, True, start)
    diag_copy.wait()


def body(stored_inverse, lhat, diag_inverse, ancestors):
    rows, cols = stored_inverse.shape
    stored = stored_inverse.reshape(rows // BLOCK, BLOCK, cols)
    anywhere = pl.BlockSpec(memory_space=pl.ANY)
    vmem = pl.BlockSpec(memory_space=pltpu.VMEM)
    smem = pl.BlockSpec(memory_space=pltpu.SMEM)
    dma = pltpu.SemaphoreType.DMA
    width = SUPERS * BLOCK
    pieces = (SIDE, SIDE, SIDE, QUARTER, BLOCK)
    gather_sems = [dma, dma((3, 3)), dma((3, 3, 3)), dma]
    tiles, diag, lists = pl.pallas_call(
        kernel,
        out_shape=(
            pltpu.VMEM((SUPERS, ANCESTORS + 1, BLOCK, BLOCK), BF16),
            pltpu.VMEM(diag_inverse.shape, BF16),
            pltpu.SMEM(ancestors.shape, jnp.int32),
        ),
        in_specs=[anywhere] * 4,
        out_specs=(vmem, vmem, smem),
        scratch_shapes=[
            pltpu.VMEM(diag_inverse.shape, BF16),
            pltpu.VMEM(pieces, BF16),
            pltpu.VMEM((rows // BLOCK, BLOCK, cols), BF16),
            pltpu.VMEM((SUPERS, ANCESTORS, SIDE, 2, QUARTER, BLOCK), BF16),
            pltpu.VMEM((SUPERS, ANCESTORS, BLOCK, BLOCK), BF16),
            pltpu.VMEM((SUPERS, SIDE, 2, QUARTER, BLOCK), BF16),
            pltpu.VMEM((SUPERS, SIDE - 1, 2, QUARTER, BLOCK), BF16),
            pltpu.VMEM((SUPERS, 2, QUARTER, BLOCK), BF16),
            pltpu.VMEM((SLOTS, QUARTER, BLOCK), BF16),
            pltpu.VMEM((PLANE, QUARTER, BLOCK), BF16),
            pltpu.VMEM(pieces, BF16),
            pltpu.VMEM((SUPERS, ANCESTORS, BLOCK, BLOCK), BF16),
            pltpu.VMEM(diag_inverse.shape, BF16),
            pltpu.VMEM((QUARTER, BLOCK), BF16),
            pltpu.VMEM(ancestors.shape, jnp.int32),
            pltpu.SMEM(ancestors.shape, jnp.int32),
            pltpu.VMEM((PIECES * PIECE, 16, 128), BF16),
            dma((4,)), dma((2,)), *gather_sems, dma, dma,
            dma, dma((SUPERS,)), dma, dma, dma, dma, dma, dma, dma, dma,
        ],
        compiler_params=pltpu.CompilerParams(
            collective_id=0, has_side_effects=True, vmem_limit_bytes=VMEM_LIMIT
        ),
        name="selected_inverse",
    )(ancestors, lhat, stored, diag_inverse)
    return pl.pallas_call(
        place,
        out_shape=(
            jax.ShapeDtypeStruct((1, rows, width), BF16),
            jax.ShapeDtypeStruct((1, cols, width), BF16),
            jax.ShapeDtypeStruct(diag_inverse.shape, BF16),
        ),
        in_specs=[smem, vmem, vmem],
        out_specs=(anywhere, anywhere, anywhere),
        scratch_shapes=[
            pltpu.VMEM((BLOCK, BLOCK), BF16),
            dma((SUPERS, ANCESTORS)), dma((SUPERS, 2)), dma,
        ],
        compiler_params=pltpu.CompilerParams(vmem_limit_bytes=VMEM_LIMIT // 8),
        name="placed_tiles",
    )(lists, tiles, diag)


def solution(mesh):
    return jax.shard_map(
        body,
        mesh=mesh,
        in_specs=(
            P("prow", "pcol"),
            P("layer", ("prow", "pcol"), None),
            P("layer", None, None, None),
            P("layer", None, None),
        ),
        out_specs=(
            P("layer", "prow", None),
            P("layer", "pcol", None),
            P("layer", None, None, None),
        ),
        check_vma=False,
    )
```

```python
import jax
import jax.numpy as jnp
from jax import lax
from jax.experimental import pallas as pl
from jax.experimental.pallas import tpu as pltpu
from jax.sharding import PartitionSpec as P

BLOCK = 256
ANCESTORS = 8
SUPERS = 2
TOP_BLOCKS = 28
SIDE = 4
PLANE = 16
PIECES = 64
QUARTER = 64
SLOTS = SUPERS * ANCESTORS
LAST = ANCESTORS - 1
MESH = pl.DeviceIdType.MESH
BF16 = jnp.bfloat16
F32 = jnp.float32
VMEM_LIMIT = 60 << 20

HOPS = (2, 1, 3)
ARRIVALS = (1, 3, 2)
NEXT = {"x": "y", "y": "z", "z": "x"}
WAY = {"x": 0, "y": 1, "z": 2}
PAIRS = sorted(((h, g) for h in ARRIVALS for g in ARRIVALS), key=lambda pair: pair.count(2))
UNIT = 16 * 128
PIECE = QUARTER * BLOCK // UNIT


class Gather:
    def __init__(self, buf, dims, me, layer, wait, send, first, second, third):
        self.buf, self.dims, self.me, self.layer, self.wait = buf, dims, me, layer, wait
        self.send, self.first, self.second, self.third = send, first, second, third

    def moved(self, **hops):
        at = dict(self.me)
        for axis, hop in hops.items():
            at[axis] = (self.me[axis] + SIDE + hop) % SIDE
        return at

    def index(self, at):
        return tuple(at[d] for d in self.dims)

    def pass_on(self, at, axis, hop, sem):
        piece = self.buf.at[self.index(at)]
        to = self.moved(**{axis: hop})
        pltpu.make_async_remote_copy(
            src_ref=piece, dst_ref=piece, send_sem=self.send, recv_sem=sem,
            device_id=(self.layer, to["x"], to["z"] * SIDE + to["y"]), device_id_type=MESH,
        ).start()

    def start(self):
        for hop in HOPS:
            for n, axis in enumerate("xyz"):
                self.pass_on(self.me, axis, hop, self.first.at[n, hop - 1])

    def after_first(self):
        for hop in ARRIVALS:
            for n, axis in enumerate("xyz"):
                self.wait(self.first.at[n, hop - 1], PIECE)
                source = self.moved(**{axis: -hop})
                for to in HOPS:
                    self.pass_on(source, NEXT[axis], to, self.second.at[n, hop - 1, to - 1])

    def after_second(self):
        for hop, then in PAIRS:
            for n, axis in enumerate("xyz"):
                self.wait(self.second.at[n, hop - 1, then - 1], PIECE)
                by = NEXT[axis]
                source = self.moved(**{axis: -hop, by: -then})
                last = next(f for f in ARRIVALS if (hop + then + f) % 3 == WAY[axis])
                self.pass_on(source, NEXT[by], last, self.third)

    def finish(self):
        self.wait(self.third, 27 * PIECE)

    def wait_sent(self):
        self.wait(self.send, (PIECES - 1) * PIECE)


def kernel(
    anc_any, panel_any, g_any, dinv_any,
    tiles, diag, anc,
    dinv, panels, g_own, g_pick, panel_t, partial, partial_in, summed, staged, moved, slots,
    other_panel_t, other_dinv, other_piece, anc_in, anc_other, measure,
    in_sem, anc_sem,
    send1, first1, second1, third1, send2, third2,
    x_send, x_recv, c_send, c_recv, a_send, a_recv, m_send, m_recv, d_send, d_recv,
):
    layer = lax.axis_index("layer")
    x = lax.axis_index("prow")
    c = lax.axis_index("pcol")
    z = c // SIDE
    y = c % SIDE
    me = {"x": x, "y": y, "z": z}
    sibling = (1 - layer, x, c)

    def wait(sem, count):
        ref = measure.at[pl.ds(0, count)]
        pltpu.make_async_copy(ref, ref, sem).wait()

    def to_sibling(src, dst, send, recv):
        return pltpu.make_async_remote_copy(
            src_ref=src, dst_ref=dst, send_sem=send, recv_sem=recv, device_id=sibling, device_id_type=MESH
        )

    barrier = pltpu.get_barrier_semaphore()
    greeted = [(layer, (x + step) % SIDE, c) for step in range(1, SIDE)]
    greeted += [(layer, x, (c + step) % PLANE) for step in range(1, PLANE)]
    greeted.append(sibling)
    for device in greeted:
        pl.semaphore_signal(barrier, inc=1, device_id=device, device_id_type=MESH)
    panel_load = pltpu.make_async_copy(panel_any, panels.at[x, z, pl.ds(y, 1)], in_sem.at[0])
    anc_load = pltpu.make_async_copy(anc_any, anc, in_sem.at[1])
    dinv_load = pltpu.make_async_copy(dinv_any, dinv, in_sem.at[2])
    g_load = pltpu.make_async_copy(g_any, g_own, in_sem.at[3])
    panel_load.start()
    anc_load.start()
    g_load.start()
    dinv_load.start()

    pl.semaphore_wait(barrier, len(greeted))

    gather1 = Gather(panels, ("x", "z", "y"), me, layer, wait, send1, first1, second1, third1)
    gather2 = Gather(slots, ("z", "y", "x"), me, layer, wait, send2, first1, second1, third2)
    panel_load.wait()
    gather1.start()
    anc_copy = to_sibling(anc_any, anc_in, anc_sem.at[0], anc_sem.at[1])
    anc_copy.start()
    anc_load.wait()
    dinv_load.wait()
    g_load.wait()

    def parent_of(k):
        return jnp.clip(anc[0, k, LAST] - TOP_BLOCKS, 0, SUPERS - 1)

    def own_super(k):
        child = jnp.where(parent_of(0) == k, 0, 1)
        return jnp.where(layer == 0, k, child)

    def slot_block(k, q):
        return jnp.where(layer == 0, anc[0, k, q], anc_other[0, k, q])

    def pick_blocks(k):
        own = own_super(k)

        def pick(p, carry):
            at = anc[0, own, p] - x * ANCESTORS
            here = jnp.logical_and(at >= 0, at < ANCESTORS)
            block = g_own[jnp.clip(at, 0, ANCESTORS - 1)]
            block = jnp.where(here, block, jnp.zeros_like(block))
            turned = block.T
            for b in range(2):
                for q in range(SIDE):
                    first = b * BLOCK + q * QUARTER
                    g_pick[k, p, q, b] = turned[first:first + QUARTER]
            return carry
        lax.fori_loop(0, ANCESTORS, pick, 0)

    def tile_of(ref, s):
        return ref[s // SIDE, s % SIDE].reshape(BLOCK, BLOCK)

    def multiply(k):
        own = own_super(k)
        total = jnp.zeros((2 * BLOCK, BLOCK), F32)
        for p in range(ANCESTORS):
            total += jnp.dot(
                g_pick[k, p].reshape(2 * BLOCK, BLOCK), tile_of(panels, own * ANCESTORS + p),
                preferred_element_type=F32,
            )
        partial[k] = total.astype(BF16).reshape(SIDE, 2, QUARTER, BLOCK)

    def start_reduce(k):
        for hop in HOPS:
            to = (x + hop) % SIDE
            pltpu.make_async_remote_copy(
                src_ref=partial.at[k, to], dst_ref=partial_in.at[k, hop - 1],
                send_sem=x_send, recv_sem=x_recv.at[k],
                device_id=(layer, to, c), device_id_type=MESH,
            ).start()

    def turn_panels():
        for k in range(SUPERS):
            def turn(p, carry):
                s = k * ANCESTORS + p
                panel_t[k, p] = tile_of(panels, s).T
                return carry
            lax.fori_loop(0, ANCESTORS, turn, 0)

    def start_move(k):
        wait(x_recv.at[k], 3 * 2 * PIECE)
        total = partial[k, x].astype(F32)
        for hop in HOPS:
            total += partial_in[k, hop - 1].astype(F32)
        summed[k] = total.astype(BF16)
        for q in range(ANCESTORS):
            staged[k * ANCESTORS + q] = summed[k, jnp.clip(slot_block(k, q) - 2 * c, 0, 1)]

        for hop in (2, 1, 3, 0):
            for row in range(2):
                to = (2 * k + row) * SIDE + (y + hop) % SIDE

                @pl.when(to != c)
                def _():
                    pltpu.make_async_remote_copy(
                        src_ref=staged.at[to], dst_ref=moved.at[c], send_sem=c_send, recv_sem=c_recv,
                        device_id=(layer, x, to), device_id_type=MESH,
                    ).start()

    def end_move():
        moved[c] = staged[c]
        wait(c_recv, (PLANE - 1) * PIECE)
        piece = moved[slot_block(c // ANCESTORS, c % ANCESTORS) // 2]
        passed = to_sibling(slots.at[z, y, x], other_piece, a_send, a_recv)

        @pl.when(layer == 0)
        def _():
            slots[z, y, x] = piece
            passed.start()

        @pl.when(layer == 1)
        def _():
            passed.wait_recv()
            edge = tile_of(panels, own_super(c // ANCESTORS) * ANCESTORS + LAST)
            new = jnp.dot(other_piece[...], edge, preferred_element_type=F32)
            slots[z, y, x] = (new - piece.astype(F32)).astype(BF16)
        return passed

    m_copy = to_sibling(panel_t, other_panel_t, m_send, m_recv)
    d_copy = to_sibling(dinv, other_dinv, d_send, d_recv)

    pick_blocks(0)
    gather1.after_first()
    gather1.after_second()
    pick_blocks(1)
    gather1.finish()
    multiply(0)
    start_reduce(0)
    multiply(1)
    start_reduce(1)
    turn_panels()

    @pl.when(layer == 0)
    def _():
        m_copy.start()
        d_copy.start()

    anc_copy.wait_recv()
    to_smem = pltpu.make_async_copy(anc_in, anc_other, in_sem.at[1])
    to_smem.start()
    to_smem.wait()
    start_move(0)
    start_move(1)
    parents, places = [], []
    for k in range(SUPERS):
        parent = parent_of(k)
        found = []
        for q in range(LAST):
            at = jnp.int32(0)
            for j in range(ANCESTORS):
                at = jnp.where(anc_other[0, parent, j] == anc[0, k, q], j, at)
            found.append(parent * ANCESTORS + at)
        parents.append(parent)
        places.append(found)

    passed = end_move()
    gather2.start()

    gather2.after_first()
    gather2.after_second()

    def matrix(a, b):
        return jnp.dot(a, b, preferred_element_type=F32)

    @pl.when(layer == 0)
    def _():
        gather2.finish()
        for k in range(SUPERS):
            total = dinv[0, k].astype(F32)
            for q in range(ANCESTORS):
                tile = tile_of(slots, k * ANCESTORS + q)
                total += matrix(panel_t[k, q], tile)
                tiles[k, q] = -tile
            diag[0, k] = total.astype(BF16)
        passed.wait_send()
        m_copy.wait_send()
        d_copy.wait_send()

    @pl.when(layer == 1)
    def _():
        m_copy.wait_recv()
        d_copy.wait_recv()
        crossed, turned = [], []
        for k in range(SUPERS):
            edge = tile_of(panels, k * ANCESTORS + LAST)
            above = other_dinv[0, parents[k]]
            crossed.append(matrix(above, edge))
            turned.append(matrix(above.T, edge))
        gather2.finish()
        for k in range(SUPERS):
            total = jnp.zeros((BLOCK, BLOCK), F32)
            for p in range(ANCESTORS):
                total += matrix(other_panel_t[parents[k], p], tile_of(slots, parents[k] * ANCESTORS + p))
            corner = (-total - crossed[k]).astype(BF16)
            tiles[k, LAST] = corner
            tiles[k, ANCESTORS] = (-total - turned[k]).astype(BF16)
            total = dinv[0, k].astype(F32)
            for q in range(LAST):
                tile = tile_of(slots, places[k][q])
                total -= matrix(panel_t[k, q], tile)
                tiles[k, q] = tile
            diag[0, k] = (total - matrix(panel_t[k, LAST], corner)).astype(BF16)

    anc_copy.wait_send()
    gather1.wait_sent()
    gather2.wait_sent()
    wait(x_send, SUPERS * 3 * 2 * PIECE)
    wait(c_send, (PLANE - 1) * PIECE)


def place(anc, tiles, diag, col_out, row_out, diag_out, zero, col_sem, row_sem, diag_sem):
    layer = lax.axis_index("layer")
    x = lax.axis_index("prow")
    c = lax.axis_index("pcol")
    zero[...] = jnp.zeros_like(zero)
    diag_copy = pltpu.make_async_copy(diag, diag_out, diag_sem)
    diag_copy.start()

    def put(out, sems, first, blocks, row_side, start):
        for k in range(SUPERS):
            for j in range(blocks):
                dst = out.at[0, pl.ds(j * BLOCK, BLOCK), pl.ds(k * BLOCK, BLOCK)]
                sem = sems.at[k, j]
                if not start:
                    pltpu.make_async_copy(zero, dst, sem).wait()
                    continue
                at = jnp.int32(0)
                hit = jnp.int32(0)
                for q in range(ANCESTORS):
                    same = anc[0, k, q] == first + j
                    at = jnp.where(same, q, at)
                    hit = jnp.where(same, 1, hit)
                if row_side:
                    turned = jnp.logical_and(layer == 1, at == ANCESTORS - 1)
                    at = jnp.where(turned, ANCESTORS, at)

                @pl.when(hit > 0)
                def _():
                    pltpu.make_async_copy(tiles.at[k, at], dst, sem).start()

                @pl.when(hit == 0)
                def _():
                    pltpu.make_async_copy(zero, dst, sem).start()

    for start in (True, False):
        put(col_out, col_sem, x * ANCESTORS, ANCESTORS, False, start)
        put(row_out, row_sem, c * 2, 2, True, start)
    diag_copy.wait()


def body(stored_inverse, lhat, diag_inverse, ancestors):
    rows, cols = stored_inverse.shape
    stored = stored_inverse.reshape(rows // BLOCK, BLOCK, cols)
    anywhere = pl.BlockSpec(memory_space=pl.ANY)
    vmem = pl.BlockSpec(memory_space=pltpu.VMEM)
    smem = pl.BlockSpec(memory_space=pltpu.SMEM)
    dma = pltpu.SemaphoreType.DMA
    width = SUPERS * BLOCK
    pieces = (SIDE, SIDE, SIDE, QUARTER, BLOCK)
    gather_sems = [dma, dma((3, 3)), dma((3, 3, 3)), dma]
    tiles, diag, lists = pl.pallas_call(
        kernel,
        out_shape=(
            pltpu.VMEM((SUPERS, ANCESTORS + 1, BLOCK, BLOCK), BF16),
            pltpu.VMEM(diag_inverse.shape, BF16),
            pltpu.SMEM(ancestors.shape, jnp.int32),
        ),
        in_specs=[anywhere] * 4,
        out_specs=(vmem, vmem, smem),
        scratch_shapes=[
            pltpu.VMEM(diag_inverse.shape, BF16),
            pltpu.VMEM(pieces, BF16),
            pltpu.VMEM((rows // BLOCK, BLOCK, cols), BF16),
            pltpu.VMEM((SUPERS, ANCESTORS, SIDE, 2, QUARTER, BLOCK), BF16),
            pltpu.VMEM((SUPERS, ANCESTORS, BLOCK, BLOCK), BF16),
            pltpu.VMEM((SUPERS, SIDE, 2, QUARTER, BLOCK), BF16),
            pltpu.VMEM((SUPERS, SIDE - 1, 2, QUARTER, BLOCK), BF16),
            pltpu.VMEM((SUPERS, 2, QUARTER, BLOCK), BF16),
            pltpu.VMEM((SLOTS, QUARTER, BLOCK), BF16),
            pltpu.VMEM((PLANE, QUARTER, BLOCK), BF16),
            pltpu.VMEM(pieces, BF16),
            pltpu.VMEM((SUPERS, ANCESTORS, BLOCK, BLOCK), BF16),
            pltpu.VMEM(diag_inverse.shape, BF16),
            pltpu.VMEM((QUARTER, BLOCK), BF16),
            pltpu.VMEM(ancestors.shape, jnp.int32),
            pltpu.SMEM(ancestors.shape, jnp.int32),
            pltpu.VMEM((PIECES * PIECE, 16, 128), BF16),
            dma((4,)), dma((2,)), *gather_sems, dma, dma,
            dma, dma((SUPERS,)), dma, dma, dma, dma, dma, dma, dma, dma,
        ],
        compiler_params=pltpu.CompilerParams(
            collective_id=0, has_side_effects=True, vmem_limit_bytes=VMEM_LIMIT
        ),
        name="selected_inverse",
    )(ancestors, lhat, stored, diag_inverse)
    return pl.pallas_call(
        place,
        out_shape=(
            jax.ShapeDtypeStruct((1, rows, width), BF16),
            jax.ShapeDtypeStruct((1, cols, width), BF16),
            jax.ShapeDtypeStruct(diag_inverse.shape, BF16),
        ),
        in_specs=[smem, vmem, vmem],
        out_specs=(anywhere, anywhere, anywhere),
        scratch_shapes=[
            pltpu.VMEM((BLOCK, BLOCK), BF16),
            dma((SUPERS, ANCESTORS)), dma((SUPERS, 2)), dma,
        ],
        compiler_params=pltpu.CompilerParams(vmem_limit_bytes=VMEM_LIMIT // 8),
        name="placed_tiles",
    )(lists, tiles, diag)


def solution(mesh):
    return jax.shard_map(
        body,
        mesh=mesh,
        in_specs=(
            P("prow", "pcol"),
            P("layer", ("prow", "pcol"), None),
            P("layer", None, None, None),
            P("layer", None, None),
        ),
        out_specs=(
            P("layer", "prow", None),
            P("layer", "pcol", None),
            P("layer", None, None, None),
        ),
        check_vma=False,
    )
```

```python
import jax
import jax.numpy as jnp
from jax import lax
from jax.experimental import pallas as pl
from jax.experimental.pallas import tpu as pltpu
from jax.sharding import PartitionSpec as P

BLOCK = 256
ANCESTORS = 8
SUPERS = 2
TOP_BLOCKS = 28
SIDE = 4
PLANE = 16
PIECES = 64
QUARTER = 64
SLOTS = SUPERS * ANCESTORS
HOLDERS = TOP_BLOCKS // 2
LAST = ANCESTORS - 1
MESH = pl.DeviceIdType.MESH
BF16 = jnp.bfloat16
F32 = jnp.float32
VMEM_LIMIT = 60 << 20

HOPS = (2, 1, 3)
ARRIVALS = (1, 3, 2)
NEXT = {"x": "y", "y": "z", "z": "x"}
WAY = {"x": 0, "y": 1, "z": 2}
PAIRS = sorted(((h, g) for h in ARRIVALS for g in ARRIVALS), key=lambda pair: pair.count(2))
UNIT = 16 * 128
PIECE = QUARTER * BLOCK // UNIT


class Gather:
    def __init__(self, buf, dims, me, layer, wait, send, first, second, third):
        self.buf, self.dims, self.me, self.layer, self.wait = buf, dims, me, layer, wait
        self.send, self.first, self.second, self.third = send, first, second, third

    def moved(self, **hops):
        at = dict(self.me)
        for axis, hop in hops.items():
            at[axis] = (self.me[axis] + SIDE + hop) % SIDE
        return at

    def index(self, at):
        return tuple(at[d] for d in self.dims)

    def pass_on(self, at, axis, hop, sem):
        piece = self.buf.at[self.index(at)]
        to = self.moved(**{axis: hop})
        pltpu.make_async_remote_copy(
            src_ref=piece, dst_ref=piece, send_sem=self.send, recv_sem=sem,
            device_id=(self.layer, to["x"], to["z"] * SIDE + to["y"]), device_id_type=MESH,
        ).start()

    def start(self):
        for hop in HOPS:
            for n, axis in enumerate("xyz"):
                self.pass_on(self.me, axis, hop, self.first.at[n, hop - 1])

    def after_first(self):
        for hop in ARRIVALS:
            for n, axis in enumerate("xyz"):
                self.wait(self.first.at[n, hop - 1], PIECE)
                source = self.moved(**{axis: -hop})
                for to in HOPS:
                    self.pass_on(source, NEXT[axis], to, self.second.at[n, hop - 1, to - 1])

    def after_second(self):
        for hop, then in PAIRS:
            for n, axis in enumerate("xyz"):
                self.wait(self.second.at[n, hop - 1, then - 1], PIECE)
                by = NEXT[axis]
                source = self.moved(**{axis: -hop, by: -then})
                last = next(f for f in ARRIVALS if (hop + then + f) % 3 == WAY[axis])
                self.pass_on(source, NEXT[by], last, self.third)

    def finish(self):
        self.wait(self.third, 27 * PIECE)

    def wait_sent(self):
        self.wait(self.send, (PIECES - 1) * PIECE)


def kernel(
    anc_any, panel_any, g_any, dinv_any,
    tiles, diag, anc,
    dinv, panels, g_own, g_pick, panel_t, partial, partial_in, summed, staged, moved, slots,
    other_panel_t, other_dinv, other_piece, anc_in, anc_other, measure,
    in_sem, anc_sem,
    send1, first1, second1, third1, send2, third2,
    x_send, x_recv, c_send, c_recv, a_send, a_recv, m_send, m_recv, d_send, d_recv, idle_sem,
):
    layer = lax.axis_index("layer")
    x = lax.axis_index("prow")
    c = lax.axis_index("pcol")
    z = c // SIDE
    y = c % SIDE
    me = {"x": x, "y": y, "z": z}
    sibling = (1 - layer, x, c)

    def wait(sem, count):
        ref = measure.at[pl.ds(0, count)]
        pltpu.make_async_copy(ref, ref, sem).wait()

    def to_sibling(src, dst, send, recv):
        return pltpu.make_async_remote_copy(
            src_ref=src, dst_ref=dst, send_sem=send, recv_sem=recv, device_id=sibling, device_id_type=MESH
        )

    barrier = pltpu.get_barrier_semaphore()
    greeted = [(layer, (x + step) % SIDE, c) for step in range(1, SIDE)]
    greeted += [(layer, x, (c + step) % PLANE) for step in range(1, PLANE)]
    greeted.append(sibling)
    for device in greeted:
        pl.semaphore_signal(barrier, inc=1, device_id=device, device_id_type=MESH)
    panel_load = pltpu.make_async_copy(panel_any, panels.at[x, z, pl.ds(y, 1)], in_sem.at[0])
    anc_load = pltpu.make_async_copy(anc_any, anc, in_sem.at[1])
    dinv_load = pltpu.make_async_copy(dinv_any, dinv, in_sem.at[2])
    g_load = pltpu.make_async_copy(g_any, g_own, in_sem.at[3])
    panel_load.start()
    anc_load.start()
    g_load.start()
    dinv_load.start()

    pl.semaphore_wait(barrier, len(greeted))

    gather1 = Gather(panels, ("x", "z", "y"), me, layer, wait, send1, first1, second1, third1)
    gather2 = Gather(slots, ("z", "y", "x"), me, layer, wait, send2, first1, second1, third2)
    panel_load.wait()
    gather1.start()
    anc_copy = to_sibling(anc_any, anc_in, anc_sem.at[0], anc_sem.at[1])
    anc_copy.start()
    anc_load.wait()
    dinv_load.wait()
    g_load.wait()

    def parent_of(k):
        return jnp.clip(anc[0, k, LAST] - TOP_BLOCKS, 0, SUPERS - 1)

    def own_super(k):
        child = jnp.where(parent_of(0) == k, 0, 1)
        return jnp.where(layer == 0, k, child)

    def slot_block(k, q):
        return jnp.where(layer == 0, anc[0, k, q], anc_other[0, k, q])

    def pick_blocks(k):
        own = own_super(k)

        def pick(p, carry):
            at = anc[0, own, p] - x * ANCESTORS
            here = jnp.logical_and(at >= 0, at < ANCESTORS)
            block = g_own[jnp.clip(at, 0, ANCESTORS - 1)]
            block = jnp.where(here, block, jnp.zeros_like(block))
            turned = block.T
            for b in range(2):
                for q in range(SIDE):
                    first = b * BLOCK + q * QUARTER
                    g_pick[k, p, q, b] = turned[first:first + QUARTER]
            return carry
        lax.fori_loop(0, ANCESTORS, pick, 0)

    def tile_of(ref, s):
        return ref[s // SIDE, s % SIDE].reshape(BLOCK, BLOCK)

    def multiply(k):
        own = own_super(k)
        total = jnp.zeros((2 * BLOCK, BLOCK), F32)
        for p in range(ANCESTORS):
            total += jnp.dot(
                g_pick[k, p].reshape(2 * BLOCK, BLOCK), tile_of(panels, own * ANCESTORS + p),
                preferred_element_type=F32,
            )
        partial[k] = total.astype(BF16).reshape(SIDE, 2, QUARTER, BLOCK)

    def start_reduce(k):
        for hop in HOPS:
            to = (x + hop) % SIDE
            pltpu.make_async_remote_copy(
                src_ref=partial.at[k, to], dst_ref=partial_in.at[k, hop - 1],
                send_sem=x_send, recv_sem=x_recv.at[k],
                device_id=(layer, to, c), device_id_type=MESH,
            ).start()

    def turn_panels():
        for k in range(SUPERS):
            def turn(p, carry):
                s = k * ANCESTORS + p
                panel_t[k, p] = tile_of(panels, s).T
                return carry
            lax.fori_loop(0, ANCESTORS, turn, 0)

    def start_move(k):
        wait(x_recv.at[k], 3 * 2 * PIECE)
        total = partial[k, x].astype(F32)
        for hop in HOPS:
            total += partial_in[k, hop - 1].astype(F32)
        summed[k] = total.astype(BF16)
        for q in range(ANCESTORS):
            staged[k * ANCESTORS + q] = summed[k, jnp.clip(slot_block(k, q) - 2 * c, 0, 1)]

        for hop in (2, 1, 3, 0):
            for row in range(2):
                to = (2 * k + row) * SIDE + (y + hop) % SIDE

                @pl.when(jnp.logical_and(to != c, c < HOLDERS))
                def _():
                    pltpu.make_async_remote_copy(
                        src_ref=staged.at[to], dst_ref=moved.at[c], send_sem=c_send, recv_sem=c_recv,
                        device_id=(layer, x, to), device_id_type=MESH,
                    ).start()

    def end_move():
        @pl.when(c < HOLDERS)
        def _():
            moved[c] = staged[c]
            wait(c_recv, (HOLDERS - 1) * PIECE)
            pl.semaphore_wait(idle_sem, PLANE - HOLDERS)

        @pl.when(c >= HOLDERS)
        def _():
            wait(c_recv, HOLDERS * PIECE)
            pl.semaphore_wait(idle_sem, PLANE - HOLDERS - 1)

        piece = moved[jnp.clip(slot_block(c // ANCESTORS, c % ANCESTORS) // 2, 0, HOLDERS - 1)]
        passed = to_sibling(slots.at[z, y, x], other_piece, a_send, a_recv)

        @pl.when(layer == 0)
        def _():
            slots[z, y, x] = piece
            passed.start()

        @pl.when(layer == 1)
        def _():
            passed.wait_recv()
            edge = tile_of(panels, own_super(c // ANCESTORS) * ANCESTORS + LAST)
            new = jnp.dot(other_piece[...], edge, preferred_element_type=F32)
            slots[z, y, x] = (new - piece.astype(F32)).astype(BF16)
        return passed

    m_copy = to_sibling(panel_t, other_panel_t, m_send, m_recv)
    d_copy = to_sibling(dinv, other_dinv, d_send, d_recv)

    pick_blocks(0)
    gather1.after_first()
    gather1.after_second()
    pick_blocks(1)
    gather1.finish()
    multiply(0)
    start_reduce(0)
    multiply(1)
    start_reduce(1)
    @pl.when(c >= HOLDERS)
    def _():
        for step in range(1, PLANE):
            pl.semaphore_signal(
                idle_sem, inc=1, device_id=(layer, x, (c + step) % PLANE), device_id_type=MESH
            )

    turn_panels()

    @pl.when(layer == 0)
    def _():
        m_copy.start()
        d_copy.start()

    anc_copy.wait_recv()
    to_smem = pltpu.make_async_copy(anc_in, anc_other, in_sem.at[1])
    to_smem.start()
    to_smem.wait()
    start_move(0)
    start_move(1)
    parents, places = [], []
    for k in range(SUPERS):
        parent = parent_of(k)
        found = []
        for q in range(LAST):
            at = jnp.int32(0)
            for j in range(ANCESTORS):
                at = jnp.where(anc_other[0, parent, j] == anc[0, k, q], j, at)
            found.append(parent * ANCESTORS + at)
        parents.append(parent)
        places.append(found)

    passed = end_move()
    gather2.start()

    gather2.after_first()
    gather2.after_second()

    def matrix(a, b):
        return jnp.dot(a, b, preferred_element_type=F32)

    @pl.when(layer == 0)
    def _():
        gather2.finish()
        for k in range(SUPERS):
            total = dinv[0, k].astype(F32)
            for q in range(ANCESTORS):
                tile = tile_of(slots, k * ANCESTORS + q)
                total += matrix(panel_t[k, q], tile)
                tiles[k, q] = -tile
            diag[0, k] = total.astype(BF16)
        passed.wait_send()
        m_copy.wait_send()
        d_copy.wait_send()

    @pl.when(layer == 1)
    def _():
        m_copy.wait_recv()
        d_copy.wait_recv()
        crossed, turned = [], []
        for k in range(SUPERS):
            edge = tile_of(panels, k * ANCESTORS + LAST)
            above = other_dinv[0, parents[k]]
            crossed.append(matrix(above, edge))
            turned.append(matrix(above.T, edge))
        gather2.finish()
        for k in range(SUPERS):
            total = jnp.zeros((BLOCK, BLOCK), F32)
            for p in range(ANCESTORS):
                total += matrix(other_panel_t[parents[k], p], tile_of(slots, parents[k] * ANCESTORS + p))
            corner = (-total - crossed[k]).astype(BF16)
            tiles[k, LAST] = corner
            tiles[k, ANCESTORS] = (-total - turned[k]).astype(BF16)
            total = dinv[0, k].astype(F32)
            for q in range(LAST):
                tile = tile_of(slots, places[k][q])
                total -= matrix(panel_t[k, q], tile)
                tiles[k, q] = tile
            diag[0, k] = (total - matrix(panel_t[k, LAST], corner)).astype(BF16)

    anc_copy.wait_send()
    gather1.wait_sent()
    gather2.wait_sent()
    wait(x_send, SUPERS * 3 * 2 * PIECE)

    @pl.when(c < HOLDERS)
    def _():
        wait(c_send, (PLANE - 1) * PIECE)


def place(anc, tiles, diag, col_out, row_out, diag_out, zero, col_sem, row_sem, diag_sem):
    layer = lax.axis_index("layer")
    x = lax.axis_index("prow")
    c = lax.axis_index("pcol")
    zero[...] = jnp.zeros_like(zero)
    diag_copy = pltpu.make_async_copy(diag, diag_out, diag_sem)
    diag_copy.start()

    def put(out, sems, first, blocks, row_side, start):
        for k in range(SUPERS):
            for j in range(blocks):
                dst = out.at[0, pl.ds(j * BLOCK, BLOCK), pl.ds(k * BLOCK, BLOCK)]
                sem = sems.at[k, j]
                if not start:
                    pltpu.make_async_copy(zero, dst, sem).wait()
                    continue
                at = jnp.int32(0)
                hit = jnp.int32(0)
                for q in range(ANCESTORS):
                    same = anc[0, k, q] == first + j
                    at = jnp.where(same, q, at)
                    hit = jnp.where(same, 1, hit)
                if row_side:
                    turned = jnp.logical_and(layer == 1, at == ANCESTORS - 1)
                    at = jnp.where(turned, ANCESTORS, at)

                @pl.when(hit > 0)
                def _():
                    pltpu.make_async_copy(tiles.at[k, at], dst, sem).start()

                @pl.when(hit == 0)
                def _():
                    pltpu.make_async_copy(zero, dst, sem).start()

    for start in (True, False):
        put(col_out, col_sem, x * ANCESTORS, ANCESTORS, False, start)
        put(row_out, row_sem, c * 2, 2, True, start)
    diag_copy.wait()


def body(stored_inverse, lhat, diag_inverse, ancestors):
    rows, cols = stored_inverse.shape
    stored = stored_inverse.reshape(rows // BLOCK, BLOCK, cols)
    anywhere = pl.BlockSpec(memory_space=pl.ANY)
    vmem = pl.BlockSpec(memory_space=pltpu.VMEM)
    smem = pl.BlockSpec(memory_space=pltpu.SMEM)
    dma = pltpu.SemaphoreType.DMA
    width = SUPERS * BLOCK
    pieces = (SIDE, SIDE, SIDE, QUARTER, BLOCK)
    gather_sems = [dma, dma((3, 3)), dma((3, 3, 3)), dma]
    tiles, diag, lists = pl.pallas_call(
        kernel,
        out_shape=(
            pltpu.VMEM((SUPERS, ANCESTORS + 1, BLOCK, BLOCK), BF16),
            pltpu.VMEM(diag_inverse.shape, BF16),
            pltpu.SMEM(ancestors.shape, jnp.int32),
        ),
        in_specs=[anywhere] * 4,
        out_specs=(vmem, vmem, smem),
        scratch_shapes=[
            pltpu.VMEM(diag_inverse.shape, BF16),
            pltpu.VMEM(pieces, BF16),
            pltpu.VMEM((rows // BLOCK, BLOCK, cols), BF16),
            pltpu.VMEM((SUPERS, ANCESTORS, SIDE, 2, QUARTER, BLOCK), BF16),
            pltpu.VMEM((SUPERS, ANCESTORS, BLOCK, BLOCK), BF16),
            pltpu.VMEM((SUPERS, SIDE, 2, QUARTER, BLOCK), BF16),
            pltpu.VMEM((SUPERS, SIDE - 1, 2, QUARTER, BLOCK), BF16),
            pltpu.VMEM((SUPERS, 2, QUARTER, BLOCK), BF16),
            pltpu.VMEM((SLOTS, QUARTER, BLOCK), BF16),
            pltpu.VMEM((HOLDERS, QUARTER, BLOCK), BF16),
            pltpu.VMEM(pieces, BF16),
            pltpu.VMEM((SUPERS, ANCESTORS, BLOCK, BLOCK), BF16),
            pltpu.VMEM(diag_inverse.shape, BF16),
            pltpu.VMEM((QUARTER, BLOCK), BF16),
            pltpu.VMEM(ancestors.shape, jnp.int32),
            pltpu.SMEM(ancestors.shape, jnp.int32),
            pltpu.VMEM((PIECES * PIECE, 16, 128), BF16),
            dma((4,)), dma((2,)), *gather_sems, dma, dma,
            dma, dma((SUPERS,)), dma, dma, dma, dma, dma, dma, dma, dma,
            pltpu.SemaphoreType.REGULAR,
        ],
        compiler_params=pltpu.CompilerParams(
            collective_id=0, has_side_effects=True, vmem_limit_bytes=VMEM_LIMIT
        ),
        name="selected_inverse",
    )(ancestors, lhat, stored, diag_inverse)
    return pl.pallas_call(
        place,
        out_shape=(
            jax.ShapeDtypeStruct((1, rows, width), BF16),
            jax.ShapeDtypeStruct((1, cols, width), BF16),
            jax.ShapeDtypeStruct(diag_inverse.shape, BF16),
        ),
        in_specs=[smem, vmem, vmem],
        out_specs=(anywhere, anywhere, anywhere),
        scratch_shapes=[
            pltpu.VMEM((BLOCK, BLOCK), BF16),
            dma((SUPERS, ANCESTORS)), dma((SUPERS, 2)), dma,
        ],
        compiler_params=pltpu.CompilerParams(vmem_limit_bytes=VMEM_LIMIT // 8),
        name="placed_tiles",
    )(lists, tiles, diag)


def solution(mesh):
    return jax.shard_map(
        body,
        mesh=mesh,
        in_specs=(
            P("prow", "pcol"),
            P("layer", ("prow", "pcol"), None),
            P("layer", None, None, None),
            P("layer", None, None),
        ),
        out_specs=(
            P("layer", "prow", None),
            P("layer", "pcol", None),
            P("layer", None, None, None),
        ),
        check_vma=False,
    )
```

```python
import jax
import jax.numpy as jnp
from jax import lax
from jax.experimental import pallas as pl
from jax.experimental.pallas import tpu as pltpu
from jax.sharding import PartitionSpec as P

BLOCK = 256
ANCESTORS = 8
SUPERS = 2
TOP_BLOCKS = 28
SIDE = 4
PLANE = 16
PIECES = 64
QUARTER = 64
SLOTS = SUPERS * ANCESTORS
HOLDERS = TOP_BLOCKS // 2
LAST = ANCESTORS - 1
MESH = pl.DeviceIdType.MESH
BF16 = jnp.bfloat16
F32 = jnp.float32
VMEM_LIMIT = 60 << 20

HOPS = (2, 1, 3)
ARRIVALS = (1, 3, 2)
NEXT = {"x": "y", "y": "z", "z": "x"}
WAY = {"x": 0, "y": 1, "z": 2}
PAIRS = sorted(((h, g) for h in ARRIVALS for g in ARRIVALS), key=lambda pair: pair.count(2))
UNIT = 16 * 128
PIECE = QUARTER * BLOCK // UNIT


class Gather:
    def __init__(self, buf, dims, me, layer, wait, send, first, second, third):
        self.buf, self.dims, self.me, self.layer, self.wait = buf, dims, me, layer, wait
        self.send, self.first, self.second, self.third = send, first, second, third

    def moved(self, **hops):
        at = dict(self.me)
        for axis, hop in hops.items():
            at[axis] = (self.me[axis] + SIDE + hop) % SIDE
        return at

    def index(self, at):
        return tuple(at[d] for d in self.dims)

    def pass_on(self, at, axis, hop, sem):
        piece = self.buf.at[self.index(at)]
        to = self.moved(**{axis: hop})
        pltpu.make_async_remote_copy(
            src_ref=piece, dst_ref=piece, send_sem=self.send, recv_sem=sem,
            device_id=(self.layer, to["x"], to["z"] * SIDE + to["y"]), device_id_type=MESH,
        ).start()

    def start(self):
        for hop in HOPS:
            for n, axis in enumerate("xyz"):
                self.pass_on(self.me, axis, hop, self.first.at[n, hop - 1])

    def after_first(self):
        for hop in ARRIVALS:
            for n, axis in enumerate("xyz"):
                self.wait(self.first.at[n, hop - 1], PIECE)
                source = self.moved(**{axis: -hop})
                for to in HOPS:
                    self.pass_on(source, NEXT[axis], to, self.second.at[n, hop - 1, to - 1])

    def after_second(self):
        for hop, then in PAIRS:
            for n, axis in enumerate("xyz"):
                self.wait(self.second.at[n, hop - 1, then - 1], PIECE)
                by = NEXT[axis]
                source = self.moved(**{axis: -hop, by: -then})
                last = next(f for f in ARRIVALS if (hop + then + f) % 3 == WAY[axis])
                self.pass_on(source, NEXT[by], last, self.third)

    def finish(self):
        self.wait(self.third, 27 * PIECE)

    def wait_sent(self):
        self.wait(self.send, (PIECES - 1) * PIECE)


def kernel(
    anc_any, panel_any, g_any, dinv_any,
    tiles, diag, anc,
    dinv, panels, g_own, g_pick, panel_t, partial, partial_in, summed, staged, moved, slots,
    other_panel_t, other_dinv, other_piece, anc_in, anc_other, measure,
    in_sem, anc_sem,
    send1, first1, second1, third1, send2, third2,
    x_send, x_recv, c_send, c_recv, a_send, a_recv, m_send, m_recv, d_send, d_recv, idle_sem,
):
    layer = lax.axis_index("layer")
    x = lax.axis_index("prow")
    c = lax.axis_index("pcol")
    z = c // SIDE
    y = c % SIDE
    me = {"x": x, "y": y, "z": z}
    sibling = (1 - layer, x, c)

    def wait(sem, count):
        ref = measure.at[pl.ds(0, count)]
        pltpu.make_async_copy(ref, ref, sem).wait()

    def to_sibling(src, dst, send, recv):
        return pltpu.make_async_remote_copy(
            src_ref=src, dst_ref=dst, send_sem=send, recv_sem=recv, device_id=sibling, device_id_type=MESH
        )

    barrier = pltpu.get_barrier_semaphore()
    greeted = [(layer, (x + step) % SIDE, c) for step in range(1, SIDE)]
    greeted += [(layer, x, (c + step) % PLANE) for step in range(1, PLANE)]
    greeted.append(sibling)
    for device in greeted:
        pl.semaphore_signal(barrier, inc=1, device_id=device, device_id_type=MESH)
    panel_load = pltpu.make_async_copy(panel_any, panels.at[x, z, pl.ds(y, 1)], in_sem.at[0])
    anc_load = pltpu.make_async_copy(anc_any, anc, in_sem.at[1])
    dinv_load = pltpu.make_async_copy(dinv_any, dinv, in_sem.at[2])
    g_load = pltpu.make_async_copy(g_any, g_own, in_sem.at[3])
    panel_load.start()
    anc_load.start()
    g_load.start()
    dinv_load.start()

    pl.semaphore_wait(barrier, len(greeted))

    gather1 = Gather(panels, ("x", "z", "y"), me, layer, wait, send1, first1, second1, third1)
    gather2 = Gather(slots, ("z", "y", "x"), me, layer, wait, send2, first1, second1, third2)
    panel_load.wait()
    gather1.start()
    anc_copy = to_sibling(anc_any, anc_in, anc_sem.at[0], anc_sem.at[1])
    anc_copy.start()
    anc_load.wait()
    dinv_load.wait()
    g_load.wait()

    def parent_of(k):
        return jnp.clip(anc[0, k, LAST] - TOP_BLOCKS, 0, SUPERS - 1)

    def own_super(k):
        child = jnp.where(parent_of(0) == k, 0, 1)
        return jnp.where(layer == 0, k, child)

    def slot_block(k, q):
        return jnp.where(layer == 0, anc[0, k, q], anc_other[0, k, q])

    def pick_blocks(k):
        own = own_super(k)

        def pick(p, carry):
            at = anc[0, own, p] - x * ANCESTORS
            here = jnp.logical_and(at >= 0, at < ANCESTORS)
            block = g_own[jnp.clip(at, 0, ANCESTORS - 1)]
            block = jnp.where(here, block, jnp.zeros_like(block))
            turned = block.T
            for b in range(2):
                for q in range(SIDE):
                    first = b * BLOCK + q * QUARTER
                    g_pick[k, p, q, b] = turned[first:first + QUARTER]
            return carry
        lax.fori_loop(0, ANCESTORS, pick, 0)

    def tile_of(ref, s):
        return ref[s // SIDE, s % SIDE].reshape(BLOCK, BLOCK)

    def multiply(k):
        own = own_super(k)
        total = jnp.zeros((2 * BLOCK, BLOCK), F32)
        for p in range(ANCESTORS):
            total += jnp.dot(
                g_pick[k, p].reshape(2 * BLOCK, BLOCK), tile_of(panels, own * ANCESTORS + p),
                preferred_element_type=F32,
            )
        partial[k] = total.astype(BF16).reshape(SIDE, 2, QUARTER, BLOCK)

    def start_reduce(k):
        for hop in HOPS:
            to = (x + hop) % SIDE
            pltpu.make_async_remote_copy(
                src_ref=partial.at[k, to], dst_ref=partial_in.at[k, hop - 1],
                send_sem=x_send, recv_sem=x_recv.at[k],
                device_id=(layer, to, c), device_id_type=MESH,
            ).start()

    def turn_panels():
        for k in range(SUPERS):
            def turn(p, carry):
                s = k * ANCESTORS + p
                panel_t[k, p] = tile_of(panels, s).T
                return carry
            lax.fori_loop(0, ANCESTORS, turn, 0)

    def start_move(k):
        wait(x_recv.at[k], 3 * 2 * PIECE)
        total = partial[k, x].astype(F32)
        for hop in HOPS:
            total += partial_in[k, hop - 1].astype(F32)
        summed[k] = total.astype(BF16)
        for q in range(ANCESTORS):
            staged[k * ANCESTORS + q] = summed[k, jnp.clip(slot_block(k, q) - 2 * c, 0, 1)]

        for hop in (2, 1, 3, 0):
            for row in range(2):
                to = (2 * k + row) * SIDE + (y + hop) % SIDE

                @pl.when(jnp.logical_and(to != c, c < HOLDERS))
                def _():
                    pltpu.make_async_remote_copy(
                        src_ref=staged.at[to], dst_ref=moved.at[c], send_sem=c_send, recv_sem=c_recv,
                        device_id=(layer, x, to), device_id_type=MESH,
                    ).start()

    def end_move():
        @pl.when(c < HOLDERS)
        def _():
            moved[c] = staged[c]
            wait(c_recv, (HOLDERS - 1) * PIECE)
            pl.semaphore_wait(idle_sem, PLANE - HOLDERS)

        @pl.when(c >= HOLDERS)
        def _():
            wait(c_recv, HOLDERS * PIECE)
            pl.semaphore_wait(idle_sem, PLANE - HOLDERS - 1)

        piece = moved[jnp.clip(slot_block(c // ANCESTORS, c % ANCESTORS) // 2, 0, HOLDERS - 1)]
        passed = to_sibling(slots.at[z, y, x], other_piece, a_send, a_recv)

        @pl.when(layer == 0)
        def _():
            slots[z, y, x] = piece
            passed.start()

        @pl.when(layer == 1)
        def _():
            passed.wait_recv()
            edge = tile_of(panels, own_super(c // ANCESTORS) * ANCESTORS + LAST)
            new = jnp.dot(other_piece[...], edge, preferred_element_type=F32)
            slots[z, y, x] = (new - piece.astype(F32)).astype(BF16)
        return passed

    m_copy = to_sibling(panel_t, other_panel_t, m_send, m_recv)
    d_copy = to_sibling(dinv, other_dinv, d_send, d_recv)

    pick_blocks(0)
    gather1.after_first()
    gather1.after_second()
    pick_blocks(1)
    gather1.finish()
    multiply(0)
    start_reduce(0)
    multiply(1)
    start_reduce(1)
    @pl.when(c >= HOLDERS)
    def _():
        for step in range(1, PLANE):
            pl.semaphore_signal(
                idle_sem, inc=1, device_id=(layer, x, (c + step) % PLANE), device_id_type=MESH
            )

    turn_panels()

    @pl.when(layer == 0)
    def _():
        m_copy.start()
        d_copy.start()

    anc_copy.wait_recv()
    to_smem = pltpu.make_async_copy(anc_in, anc_other, in_sem.at[1])
    to_smem.start()
    to_smem.wait()
    start_move(0)
    start_move(1)
    parents, places = [], []
    for k in range(SUPERS):
        parent = parent_of(k)
        found = []
        for q in range(LAST):
            at = jnp.int32(0)
            for j in range(ANCESTORS):
                at = jnp.where(anc_other[0, parent, j] == anc[0, k, q], j, at)
            found.append(parent * ANCESTORS + at)
        parents.append(parent)
        places.append(found)

    passed = end_move()
    gather2.start()

    gather2.after_first()
    gather2.after_second()

    def matrix(a, b):
        return jnp.dot(a, b, preferred_element_type=F32)

    @pl.when(layer == 0)
    def _():
        gather2.finish()
        for k in range(SUPERS):
            total = dinv[0, k].astype(F32)
            for q in range(ANCESTORS):
                tile = tile_of(slots, k * ANCESTORS + q)
                total += matrix(panel_t[k, q], tile)
                tiles[k, q] = -tile
            diag[0, k] = total.astype(BF16)
        passed.wait_send()
        m_copy.wait_send()
        d_copy.wait_send()

    @pl.when(layer == 1)
    def _():
        m_copy.wait_recv()
        d_copy.wait_recv()
        crossed, turned, corners = [], [], []
        for k in range(SUPERS):
            edge = tile_of(panels, k * ANCESTORS + LAST)
            above = other_dinv[0, parents[k]]
            crossed.append(matrix(above, edge))
            turned.append(matrix(above.T, edge))
        gather2.finish()
        for k in range(SUPERS):
            total = jnp.zeros((BLOCK, BLOCK), F32)
            for p in range(ANCESTORS):
                total += matrix(other_panel_t[parents[k], p], tile_of(slots, parents[k] * ANCESTORS + p))
            corner = (-total - crossed[k]).astype(BF16)
            tiles[k, LAST] = corner
            tiles[k, ANCESTORS] = (-total - turned[k]).astype(BF16)
            corners.append(corner)
        for k in range(SUPERS):
            total = dinv[0, k].astype(F32)
            for q in range(LAST):
                tile = tile_of(slots, places[k][q])
                total -= matrix(panel_t[k, q], tile)
                tiles[k, q] = tile
            diag[0, k] = (total - matrix(panel_t[k, LAST], corners[k])).astype(BF16)

    anc_copy.wait_send()
    gather1.wait_sent()
    gather2.wait_sent()
    wait(x_send, SUPERS * 3 * 2 * PIECE)

    @pl.when(c < HOLDERS)
    def _():
        wait(c_send, (PLANE - 1) * PIECE)


def place(anc, tiles, diag, col_out, row_out, diag_out, zero, col_sem, row_sem, diag_sem):
    layer = lax.axis_index("layer")
    x = lax.axis_index("prow")
    c = lax.axis_index("pcol")
    zero[...] = jnp.zeros_like(zero)
    diag_copy = pltpu.make_async_copy(diag, diag_out, diag_sem)
    diag_copy.start()

    def put(out, sems, first, blocks, row_side, start):
        for k in range(SUPERS):
            for j in range(blocks):
                dst = out.at[0, pl.ds(j * BLOCK, BLOCK), pl.ds(k * BLOCK, BLOCK)]
                sem = sems.at[k, j]
                if not start:
                    pltpu.make_async_copy(zero, dst, sem).wait()
                    continue
                at = jnp.int32(0)
                hit = jnp.int32(0)
                for q in range(ANCESTORS):
                    same = anc[0, k, q] == first + j
                    at = jnp.where(same, q, at)
                    hit = jnp.where(same, 1, hit)
                if row_side:
                    turned = jnp.logical_and(layer == 1, at == ANCESTORS - 1)
                    at = jnp.where(turned, ANCESTORS, at)

                @pl.when(hit > 0)
                def _():
                    pltpu.make_async_copy(tiles.at[k, at], dst, sem).start()

                @pl.when(hit == 0)
                def _():
                    pltpu.make_async_copy(zero, dst, sem).start()

    for start in (True, False):
        put(col_out, col_sem, x * ANCESTORS, ANCESTORS, False, start)
        put(row_out, row_sem, c * 2, 2, True, start)
    diag_copy.wait()


def body(stored_inverse, lhat, diag_inverse, ancestors):
    rows, cols = stored_inverse.shape
    stored = stored_inverse.reshape(rows // BLOCK, BLOCK, cols)
    anywhere = pl.BlockSpec(memory_space=pl.ANY)
    vmem = pl.BlockSpec(memory_space=pltpu.VMEM)
    smem = pl.BlockSpec(memory_space=pltpu.SMEM)
    dma = pltpu.SemaphoreType.DMA
    width = SUPERS * BLOCK
    pieces = (SIDE, SIDE, SIDE, QUARTER, BLOCK)
    gather_sems = [dma, dma((3, 3)), dma((3, 3, 3)), dma]
    tiles, diag, lists = pl.pallas_call(
        kernel,
        out_shape=(
            pltpu.VMEM((SUPERS, ANCESTORS + 1, BLOCK, BLOCK), BF16),
            pltpu.VMEM(diag_inverse.shape, BF16),
            pltpu.SMEM(ancestors.shape, jnp.int32),
        ),
        in_specs=[anywhere] * 4,
        out_specs=(vmem, vmem, smem),
        scratch_shapes=[
            pltpu.VMEM(diag_inverse.shape, BF16),
            pltpu.VMEM(pieces, BF16),
            pltpu.VMEM((rows // BLOCK, BLOCK, cols), BF16),
            pltpu.VMEM((SUPERS, ANCESTORS, SIDE, 2, QUARTER, BLOCK), BF16),
            pltpu.VMEM((SUPERS, ANCESTORS, BLOCK, BLOCK), BF16),
            pltpu.VMEM((SUPERS, SIDE, 2, QUARTER, BLOCK), BF16),
            pltpu.VMEM((SUPERS, SIDE - 1, 2, QUARTER, BLOCK), BF16),
            pltpu.VMEM((SUPERS, 2, QUARTER, BLOCK), BF16),
            pltpu.VMEM((SLOTS, QUARTER, BLOCK), BF16),
            pltpu.VMEM((HOLDERS, QUARTER, BLOCK), BF16),
            pltpu.VMEM(pieces, BF16),
            pltpu.VMEM((SUPERS, ANCESTORS, BLOCK, BLOCK), BF16),
            pltpu.VMEM(diag_inverse.shape, BF16),
            pltpu.VMEM((QUARTER, BLOCK), BF16),
            pltpu.VMEM(ancestors.shape, jnp.int32),
            pltpu.SMEM(ancestors.shape, jnp.int32),
            pltpu.VMEM((PIECES * PIECE, 16, 128), BF16),
            dma((4,)), dma((2,)), *gather_sems, dma, dma,
            dma, dma((SUPERS,)), dma, dma, dma, dma, dma, dma, dma, dma,
            pltpu.SemaphoreType.REGULAR,
        ],
        compiler_params=pltpu.CompilerParams(
            collective_id=0, has_side_effects=True, vmem_limit_bytes=VMEM_LIMIT
        ),
        name="selected_inverse",
    )(ancestors, lhat, stored, diag_inverse)
    return pl.pallas_call(
        place,
        out_shape=(
            jax.ShapeDtypeStruct((1, rows, width), BF16),
            jax.ShapeDtypeStruct((1, cols, width), BF16),
            jax.ShapeDtypeStruct(diag_inverse.shape, BF16),
        ),
        in_specs=[smem, vmem, vmem],
        out_specs=(anywhere, anywhere, anywhere),
        scratch_shapes=[
            pltpu.VMEM((BLOCK, BLOCK), BF16),
            dma((SUPERS, ANCESTORS)), dma((SUPERS, 2)), dma,
        ],
        compiler_params=pltpu.CompilerParams(vmem_limit_bytes=VMEM_LIMIT // 8),
        name="placed_tiles",
    )(lists, tiles, diag)


def solution(mesh):
    return jax.shard_map(
        body,
        mesh=mesh,
        in_specs=(
            P("prow", "pcol"),
            P("layer", ("prow", "pcol"), None),
            P("layer", None, None, None),
            P("layer", None, None),
        ),
        out_specs=(
            P("layer", "prow", None),
            P("layer", "pcol", None),
            P("layer", None, None, None),
        ),
        check_vma=False,
    )
```
